128 devices in a mesh: head: 4 (over z_hi, core), freq: 32 (over y, x, z_lo).
Axes of the slice: x: 4, y: 4, z: 4 (z_hi: 2, z_lo: 2; z = z_hi * 2 + z_lo), core: 2. Of those that a mesh axis runs over, the one named last changes fastest.
Arguments:
- transfer: bfloat16 [2, 36, 256, 65536], P(None, 'head', None, 'freq'), may hold values from -6 to 6
- amplitudes: float32 [2, 36, 65536], P(None, 'head', 'freq'), may hold values from -0.00390625 to 0.00390625
- weights: float32 [36], P('head'), may hold values from 0.2 to 2
Outputs:
- stress: float32 [256, 256, 256], P('head', 'freq')
The draws below stay inside these ranges and needn't reach their ends.
All inputs are finite; a program needn't handle non-finite values.
Results may differ from the reference program's by a relative error of at most 0.0036.
Values may be sent and summed in bfloat16 or wider, within the bound.
A program may use at most 128 MiB of HBM per device.

```python
import math
import jax
import jax.numpy as jnp
from jax import lax

HEADINGS = 36
NA = 256
NB = 256
SPOTS = 256
NF = 65536


def block_levels(key, extent, cuts, low, largest):
    factor_of = 1.0
    for position, shards_of in cuts:
        heights = jax.random.uniform(jax.random.fold_in(jax.random.fold_in(key, 6), position), (shards_of,), jnp.float32, low / len(cuts), largest / len(cuts))
        factor_of = factor_of * jnp.repeat(jnp.exp(heights), extent[position] // shards_of).reshape((-1,) + (1,) * (len(extent) - 1 - position))
    return factor_of


def centred(key, shape, spread, reach, pieces=(), kind=jnp.bfloat16):
    values = jax.random.normal(key, shape, jnp.float32) * spread
    if len(pieces) > 0:
        values = block_levels(key, shape, pieces, -0.22, 0.18) * values
    return jnp.clip(values, min=-reach, max=reach).astype(kind)


def setup_inputs(seed: int = 0) -> dict:
    keys = jax.random.split(jax.random.key(seed), 4)
    transfer = centred(keys[0], (2, HEADINGS, SPOTS, NF), 1.0, 6.0, ((1, 4), (3, 32)))
    amplitudes = centred(keys[1], (2, HEADINGS, NF), (HEADINGS * NA * NB) ** -0.5, 0.00390625, ((1, 4), (2, 32)), jnp.float32)
    weights = jnp.clip(jnp.exp(math.log(2.0) - 2.3025851 * jax.random.uniform(keys[2], (HEADINGS,), jnp.float32) ** block_levels(keys[2], (HEADINGS,), ((0, 4),), -0.2, 0.2)), 0.2, 2.0)
    return dict(transfer=transfer, amplitudes=amplitudes, weights=weights)


def reference(transfer, amplitudes, weights):
    weighted = weights[None, :, None] * amplitudes

    def add_heading(heading, totals):
        layer = lax.dynamic_index_in_dim(transfer, heading, 1, keepdims=False).astype(jnp.float32)
        factor = lax.dynamic_index_in_dim(weighted, heading, 1, keepdims=False)
        real_part = totals[0] + layer[0] * factor[0][None, :] - layer[1] * factor[1][None, :]
        imag_part = totals[1] + layer[0] * factor[1][None, :] + layer[1] * factor[0][None, :]
        return jnp.stack([real_part, imag_part])

    spectrum = lax.fori_loop(0, HEADINGS, add_heading, jnp.zeros((2, SPOTS, NA * NB), jnp.float32))
    spectrum = spectrum.astype(jnp.bfloat16)
    grid = spectrum.reshape(2, SPOTS, NA, NB).astype(jnp.float32)

    positions = jnp.arange(NA, dtype=jnp.int32)
    angles = ((positions[:, None] * positions[None, :]) % NA).astype(jnp.float32) * (2.0 * math.pi / NA)
    cos_one = lax.optimization_barrier(jnp.cos(angles).astype(jnp.bfloat16)).astype(jnp.float32)
    sin_one = lax.optimization_barrier(jnp.sin(angles).astype(jnp.bfloat16)).astype(jnp.float32)
    sectioned_real = jnp.einsum('sab,at->sbt', grid[0], cos_one) - jnp.einsum('sab,at->sbt', grid[1], sin_one)
    sectioned_imag = jnp.einsum('sab,at->sbt', grid[0], sin_one) + jnp.einsum('sab,at->sbt', grid[1], cos_one)

    bin_index = jnp.arange(NB, dtype=jnp.int32)
    time_index = jnp.arange(NA, dtype=jnp.int32)
    products = (bin_index[:, None] * time_index[None, :]) % (NA * NB)
    twist = products.astype(jnp.float32) * (2.0 * math.pi / (NA * NB))
    cos_vals = jnp.cos(twist)
    sin_vals = jnp.sin(twist)
    turned_real = sectioned_real * cos_vals[None] - sectioned_imag * sin_vals[None]
    turned_imag = sectioned_real * sin_vals[None] + sectioned_imag * cos_vals[None]

    angles_two = ((bin_index[:, None] * bin_index[None, :]) % NB).astype(jnp.float32) * (2.0 * math.pi / NB)
    cos_two = jnp.cos(angles_two)
    sin_two = jnp.sin(angles_two)
    stress = jnp.einsum('sbt,bu->stu', turned_real, cos_two, precision=lax.Precision.HIGHEST)
    stress = stress - jnp.einsum('sbt,bu->stu', turned_imag, sin_two, precision=lax.Precision.HIGHEST)
    return stress
```

```python
import functools
import math

import jax
import jax.numpy as jnp
import ml_dtypes
import numpy as np
from jax import lax
from jax.experimental import pallas as pl
from jax.experimental.pallas import tpu as pltpu
from jax.sharding import PartitionSpec as P

N = 256
HALF = N // 2
HEADS = 9
SPOTS = 64
FREQ = 32
AL = 8
PL = 4
SLOTS = 8
MESH = pl.DeviceIdType.MESH


def tables():
    n = np.arange(N)
    angle = 2.0 * math.pi * ((n[:, None] * n[None, :]) % N) / N
    trig = np.stack([np.cos(angle), np.sin(angle)])
    trig = trig.reshape(2, N, FREQ, AL)
    first = np.zeros((2, 2, N, FREQ, 2, AL))
    for i in range(2):
        first[i, :, :, :, i, :] = trig
    first = first.reshape(4 * N, 2 * N).astype(ml_dtypes.bfloat16)
    order = np.zeros((2, HALF, HALF))
    order[0] = np.eye(HALF)
    order[1][np.arange(HALF), (HALF - np.arange(HALF)) % HALF] = 1.0
    order = order.astype(ml_dtypes.bfloat16)
    pairs = np.arange(HALF)
    mirror = np.where(pairs == 0, HALF, N - pairs)
    low = np.stack([pairs, mirror])
    turn = 2.0 * math.pi * ((low[:, :, None] * n) % (N * N)) / (N * N)
    cos_turn, sin_turn = np.cos(turn), np.sin(turn)
    cos_turn[1, 0], sin_turn[1, 0] = -np.sin(turn[1, 0]), np.cos(turn[1, 0])
    twist = np.stack([cos_turn, sin_turn], axis=2)
    twist = twist.reshape(2, FREQ, PL, 2, N).transpose(1, 4, 0, 2, 3).reshape(FREQ, N, 4 * PL)
    wide = np.zeros((FREQ, N, 128), np.float32)
    wide[:, :, : 4 * PL] = twist
    cos_two, sin_two = np.cos(angle)[:HALF], -np.sin(angle)[:HALF]
    sin_two[0] = -((-1.0) ** n)
    second = np.concatenate([cos_two, sin_two], axis=1).astype(np.float32)
    upper = second.astype(ml_dtypes.bfloat16)
    lower = (second - upper.astype(np.float32)).astype(ml_dtypes.bfloat16)
    second = np.concatenate([upper, lower], axis=0)
    return first, order, wide, second


def kernel(
    transfer, amplitudes, weights, first, order, twist, second,
    out,
    slabs, amp, wide, part, core_in, pair_out, pair_in, gather, bins_out, bins_in,
    first_v, order_v, twist_v, second_v, turn, passed, folded, fold_out, fold_in, fold_f32, staged,
    slab_sem, const_sem, core_send, core_recv, pair_send, pair_recv,
    bins_send, bins_recv, fold_send, fold_recv,
):
    head = lax.axis_index("head")
    me = lax.axis_index("freq")
    z, core = head // 2, lax.rem(head, 2)
    other_core = (z * 2 + 1 - core, me)
    other_z = ((1 - z) * 2 + core, me)
    f32, bf16 = jnp.float32, jnp.bfloat16

    def slab_copy(i):
        far, role, digit = i // 16, lax.rem(i // 8, 2), lax.rem(i, 8)
        half = jnp.where(far == 0, 1 - z, z)
        rows = pl.ds(pl.multiple_of(half * 128, 128), 128)
        lanes = pl.ds(pl.multiple_of(digit * N + role * HALF, 128), 128)
        slot = lax.rem(i, SLOTS)
        return pltpu.make_async_copy(
            transfer.at[:, :, rows, lanes], slabs.at[slot], slab_sem.at[slot]
        )

    consts = [
        pltpu.make_async_copy(amplitudes, amp, const_sem.at[0]),
        pltpu.make_async_copy(first, first_v, const_sem.at[1]),
        pltpu.make_async_copy(order, order_v, const_sem.at[2]),
        pltpu.make_async_copy(twist.at[me], twist_v, const_sem.at[3]),
        pltpu.make_async_copy(second, second_v, const_sem.at[4]),
    ]
    consts[0].start()

    @pl.loop(0, SLOTS)
    def _(i):
        slab_copy(i).start()

    barrier = pltpu.get_barrier_semaphore()

    @pl.loop(1, FREQ)
    def _(d):
        pl.semaphore_signal(
            barrier, inc=1, device_id=(head, lax.rem(me + d, FREQ)), device_id_type=MESH
        )

    pl.semaphore_signal(barrier, inc=1, device_id=other_core, device_id_type=MESH)
    pl.semaphore_signal(barrier, inc=1, device_id=other_z, device_id_type=MESH)

    consts[0].wait()
    for r in range(2):
        for h in range(HEADS):
            row = amp[r, h : h + 1, :] * weights[h]
            wide[r, h] = jnp.broadcast_to(row, (8, row.shape[1]))

    def add_headings(chunk):
        @pl.loop(0, 4)
        def _(s):
            i = chunk * 4 + s
            role, digit = lax.rem(i // 8, 2), lax.rem(i, 8)
            lanes = pl.ds(pl.multiple_of(digit * N + role * HALF, 128), 128)
            slot = lax.rem(i, SLOTS)
            slab_copy(i).wait()

            @pl.loop(0, 2)
            def _(mine):
                row = jnp.where(mine == 0, 1 - core, core) * SPOTS
                for tile in range(SPOTS // 16):
                    rows = pl.ds(pl.multiple_of(row + tile * 16, 16), 16)
                    real = imag = None
                    for h in range(HEADS):
                        tr = slabs[slot, 0, h, rows, :].astype(f32).reshape(2, 8, 128)
                        ti = slabs[slot, 1, h, rows, :].astype(f32).reshape(2, 8, 128)
                        wr = wide[0, h, :, lanes][None]
                        wi = wide[1, h, :, lanes][None]
                        re, im = tr * wr - ti * wi, tr * wi + ti * wr
                        real = re if real is None else real + re
                        imag = im if imag is None else imag + im
                    part[mine, chunk, s, tile * 16 : tile * 16 + 16, :] = real.reshape(16, 128)
                    part[mine, chunk, s, SPOTS + tile * 16 : SPOTS + tile * 16 + 16, :] = (
                        imag.reshape(16, 128)
                    )

            @pl.when(i + SLOTS < 32)
            def _():
                slab_copy(i + SLOTS).start()

    def core_copy(chunk):
        return pltpu.make_async_remote_copy(
            src_ref=part.at[0, chunk], dst_ref=core_in.at[chunk],
            send_sem=core_send.at[chunk], recv_sem=core_recv.at[chunk],
            device_id=other_core, device_id_type=MESH,
        )

    def pair_copy(chunk):
        return pltpu.make_async_remote_copy(
            src_ref=pair_out.at[chunk], dst_ref=pair_in.at[chunk],
            send_sem=pair_send.at[chunk], recv_sem=pair_recv.at[chunk],
            device_id=other_z, device_id_type=MESH,
        )

    def send_pair(chunk):
        core_copy(chunk).wait_recv()

        @pl.loop(0, 4)
        def _(s):
            pair_out[chunk, s] = (part[1, chunk, s] + core_in[chunk, s]).astype(bf16)

        pair_copy(chunk).start()

    for chunk in range(8):
        add_headings(chunk)
        if chunk == 0:
            pl.semaphore_wait(barrier, FREQ + 1)
        core_copy(chunk).start()
        if 1 <= chunk <= 4:
            send_pair(chunk - 1)
        if chunk == 4:
            for c in consts[1:]:
                c.start()

    for c in consts[1:]:
        c.wait()

    def send_bins(role):
        for half in range(2):
            chunk = role * 2 + half
            core_copy(4 + chunk).wait_recv()
            pair_copy(chunk).wait_recv()
            for s in range(4):
                value = part[1, 4 + chunk, s] + core_in[4 + chunk, s]
                value = (value + pair_in[chunk, s].astype(f32)).astype(bf16)
                moved = lax.dot_general(
                    order_v[role], value, (((1,), (1,)), ((), ())), preferred_element_type=f32
                )
                gather[role, pl.ds(half * 4 + s, HALF, stride=AL), :] = moved
        bins_out[role] = gather[role].reshape(FREQ, PL * AL, 128).astype(bf16)

        @pl.loop(1, FREQ)
        def _(d):
            to = lax.rem(me + d, FREQ)
            pltpu.make_async_remote_copy(
                src_ref=bins_out.at[role, to], dst_ref=bins_in.at[role, me],
                send_sem=bins_send.at[role], recv_sem=bins_recv.at[role],
                device_id=(head, to), device_id_type=MESH,
            ).start()

        bins_in[role, me] = bins_out[role, me]

    def all_but_one(ref, sem):
        return pltpu.make_async_copy(ref.at[pl.ds(0, FREQ - 1)], ref.at[pl.ds(0, FREQ - 1)], sem)

    send_bins(0)
    for i in range(4 * PL):
        turn[i] = jnp.broadcast_to(twist_v[:, i : i + 1], (N, 128))
    send_bins(1)

    lane = lax.broadcasted_iota(jnp.int32, (1, 128), 1)
    low = lane < SPOTS
    sign = jnp.where(low, -1.0, 1.0).astype(f32)
    lone = jnp.where(me == 0, 0.0, 1.0).astype(f32)
    ones = jnp.ones((1, 128), f32)
    scale = [
        [jnp.where(low, ones, lone)] + [ones] * (PL - 1),
        [jnp.where(low, lone, -ones)] + [-sign] * (PL - 1),
    ]

    for role in range(2):
        all_but_one(bins_in.at[role], bins_recv.at[role]).wait()
        both = jnp.concatenate(
            [bins_in[role, :, i * 16 : i * 16 + 16, :].reshape(2 * N, 128) for i in range(2)],
            axis=1,
        )
        for p2 in range(2):
            passed[...] = jnp.dot(
                first_v[p2 * 2 * N : (p2 + 1) * 2 * N, :], both, preferred_element_type=f32
            )
            for i in range(2):
                p = i * 2 + p2
                column = (role * PL + p) * 2

                @pl.loop(0, 4)
                def _(block):
                    rows = pl.ds(pl.multiple_of(block * 64, 64), 64)
                    more = pl.ds(pl.multiple_of(N + block * 64, 64), 64)
                    lanes = slice(i * 128, i * 128 + 128)
                    c, s = passed[rows, lanes], passed[more, lanes]
                    cw, sw = turn[column, rows, :], turn[column + 1, rows, :]
                    value = (c * cw - s * sw) + sign * pltpu.roll(s * cw + c * sw, SPOTS, 1)
                    value = (value * scale[role][p]).reshape(8, AL, 128)
                    times = pl.ds(pl.multiple_of(block * 8, 8), 8)
                    place = (times, slice(p * AL, (p + 1) * AL), slice(None))
                    if role == 0:
                        folded[place] = value
                    else:
                        folded[place] = folded[place] + value

    fold_out[...] = folded[...].astype(bf16)

    @pl.loop(1, FREQ)
    def _(d):
        to = lax.rem(me + d, FREQ)
        pltpu.make_async_remote_copy(
            src_ref=fold_out.at[to], dst_ref=fold_in.at[me],
            send_sem=fold_send.at[0], recv_sem=fold_recv.at[0],
            device_id=(head, to), device_id_type=MESH,
        ).start()

    fold_in[me] = fold_out[me]
    for chunk in range(8):
        core_copy(chunk).wait_send()
    for chunk in range(4):
        pair_copy(chunk).wait_send()
    for role in range(2):
        all_but_one(bins_out.at[role], bins_send.at[role]).wait()
    all_but_one(fold_in, fold_recv.at[0]).wait()

    fold_f32[...] = fold_in[...].astype(f32).reshape(FREQ * PL * AL, 128)
    for t in range(AL):
        value = fold_f32[pl.ds(t, HALF, stride=AL), :].astype(bf16)
        value = jnp.concatenate([value, value], axis=0)
        result = lax.dot_general(
            value, second_v[...], (((0,), (0,)), ((), ())), preferred_element_type=f32
        )
        result = result[:SPOTS, :N] + result[SPOTS:, N:]
        for i in range(2):
            staged[i, pl.ds(t, SPOTS, stride=AL), :] = result[:, i * 128 : i * 128 + 128]
    for i in range(2):
        out[:, i * 128 : i * 128 + 128] = staged[i]
    all_but_one(fold_out, fold_send.at[0]).wait()


def on_device(transfer, amplitudes, weights):
    f32, bf16 = jnp.float32, jnp.bfloat16
    any_spec = pl.BlockSpec(memory_space=pl.ANY)
    stress = pl.pallas_call(
        kernel,
        out_shape=jax.ShapeDtypeStruct((SPOTS * AL, N), f32),
        in_specs=[any_spec, any_spec, pl.BlockSpec(memory_space=pltpu.SMEM)] + [any_spec] * 4,
        out_specs=pl.BlockSpec(memory_space=pltpu.VMEM),
        scratch_shapes=[
            pltpu.VMEM((SLOTS, 2, HEADS, 128, 128), bf16),
            pltpu.VMEM((2, HEADS, AL * N), f32),
            pltpu.VMEM((2, HEADS, 8, AL * N), f32),
            pltpu.VMEM((2, 8, 4, 128, 128), f32),
            pltpu.VMEM((8, 4, 128, 128), f32),
            pltpu.VMEM((4, 4, 128, 128), bf16),
            pltpu.VMEM((4, 4, 128, 128), bf16),
            pltpu.VMEM((2, HALF * AL, 128), f32),
            pltpu.VMEM((2, FREQ, PL * AL, 128), bf16),
            pltpu.VMEM((2, FREQ, PL * AL, 128), bf16),
            pltpu.VMEM((4 * N, 2 * N), bf16),
            pltpu.VMEM((2, HALF, HALF), bf16),
            pltpu.VMEM((N, 128), f32),
            pltpu.VMEM((N, 2 * N), bf16),
            pltpu.VMEM((4 * PL, N, 128), f32),
            pltpu.VMEM((2 * N, N), f32),
            pltpu.VMEM((FREQ, PL * AL, 128), f32),
            pltpu.VMEM((FREQ, PL * AL, 128), bf16),
            pltpu.VMEM((FREQ, PL * AL, 128), bf16),
            pltpu.VMEM((FREQ * PL * AL, 128), f32),
            pltpu.VMEM((2, SPOTS * AL, 128), f32),
            pltpu.SemaphoreType.DMA((SLOTS,)),
            pltpu.SemaphoreType.DMA((5,)),
            pltpu.SemaphoreType.DMA((8,)),
            pltpu.SemaphoreType.DMA((8,)),
            pltpu.SemaphoreType.DMA((4,)),
            pltpu.SemaphoreType.DMA((4,)),
            pltpu.SemaphoreType.DMA((2,)),
            pltpu.SemaphoreType.DMA((2,)),
            pltpu.SemaphoreType.DMA((1,)),
            pltpu.SemaphoreType.DMA((1,)),
        ],
        compiler_params=pltpu.CompilerParams(
            collective_id=0, has_side_effects=True, vmem_limit_bytes=56 * 2**20
        ),
        cost_estimate=pl.CostEstimate(
            flops=900_000_000, bytes_accessed=22_000_000, transcendentals=0
        ),
    )(transfer, amplitudes, weights, *[jnp.asarray(table) for table in tables()])
    return stress.reshape(SPOTS, AL, N)


def solution(mesh):
    in_specs = (P(None, "head", None, "freq"), P(None, "head", "freq"), P("head"))
    out_specs = P("head", "freq", None)
    return jax.shard_map(
        on_device, mesh=mesh, in_specs=in_specs, out_specs=out_specs, check_vma=False
    )
```

```python
import functools
import math

import jax
import jax.numpy as jnp
import ml_dtypes
import numpy as np
from jax import lax
from jax.experimental import pallas as pl
from jax.experimental.pallas import tpu as pltpu
from jax.sharding import PartitionSpec as P

N = 256
HALF = N // 2
HEADS = 9
SPOTS = 64
FREQ = 32
AL = 8
PL = 4
EARLY = 2
LATE = PL - EARLY
SLOTS = 8
MESH = pl.DeviceIdType.MESH


def tables():
    n = np.arange(N)
    angle = 2.0 * math.pi * ((n[:, None] * n[None, :]) % N) / N
    trig = np.stack([np.cos(angle), np.sin(angle)])
    trig = trig.reshape(2, N, FREQ, AL)
    first = np.zeros((2, 2, N, FREQ, 2, AL))
    for i in range(2):
        first[i, :, :, :, i, :] = trig
    first = first.reshape(4 * N, 2 * N).astype(ml_dtypes.bfloat16)
    pairs = HALF // PL * np.arange(PL) + np.arange(FREQ)[:, None]
    rows = np.concatenate([pairs[:, :EARLY].reshape(-1), pairs[:, EARLY:].reshape(-1)])
    order = np.zeros((2, HALF, HALF))
    order[0][np.arange(HALF), rows] = 1.0
    order[1][np.arange(HALF), (HALF - rows) % HALF] = 1.0
    order = order.astype(ml_dtypes.bfloat16)
    pairs = pairs.reshape(-1)
    mirror = np.where(pairs == 0, HALF, N - pairs)
    low = np.stack([pairs, mirror])
    turn = 2.0 * math.pi * ((low[:, :, None] * n) % (N * N)) / (N * N)
    cos_turn, sin_turn = np.cos(turn), np.sin(turn)
    cos_turn[1, 0], sin_turn[1, 0] = -np.sin(turn[1, 0]), np.cos(turn[1, 0])
    twist = np.stack([cos_turn, sin_turn], axis=2)
    twist = twist.reshape(2, FREQ, PL, 2, N).transpose(1, 4, 0, 2, 3).reshape(FREQ, N, 4 * PL)
    wide = np.zeros((FREQ, N, 128), np.float32)
    wide[:, :, : 4 * PL] = twist
    cos_two, sin_two = np.cos(angle)[:HALF], -np.sin(angle)[:HALF]
    sin_two[0] = -((-1.0) ** n)
    second = np.concatenate([cos_two, sin_two], axis=1).astype(np.float32)[pairs]
    upper = second.astype(ml_dtypes.bfloat16)
    lower = (second - upper.astype(np.float32)).astype(ml_dtypes.bfloat16)
    second = np.concatenate([upper, lower], axis=0)
    return first, order, wide, second


def farthest_first():
    steps = [(y, x, z) for y in range(4) for x in range(4) for z in range(2)]
    return sorted(steps, key=lambda d: -(min(d[0], 4 - d[0]) + min(d[1], 4 - d[1]) + d[2]))[:-1]


def kernel(
    transfer, amplitudes, weights, first, order, twist,
    out,
    slabs, amp, wide, part, core_in, pair_out, pair_in, early_own, gather_early, gather_late,
    early_out, early_in, late_out, late_in,
    first_v, order_v, twist_v, turn, passed, folded, late_folded, cross_out, cross_in,
    fold_out, fold_in,
    slab_sem, const_sem, core_send, core_recv, pair_send, pair_recv,
    bins_send, bins_recv, cross_send, cross_recv, fold_send, fold_recv,
):
    head = lax.axis_index("head")
    me = lax.axis_index("freq")
    z, core = head // 2, lax.rem(head, 2)
    other_core = (z * 2 + 1 - core, me)
    other_z = ((1 - z) * 2 + core, me)
    f32, bf16 = jnp.float32, jnp.bfloat16
    y, x, z_low = me // 8, lax.rem(me // 2, 4), lax.rem(me, 2)
    others = [
        lax.rem(y + dy, 4) * 8 + lax.rem(x + dx, 4) * 2 + lax.rem(z_low + dz, 2)
        for dy, dx, dz in farthest_first()
    ]

    def slab_copy(i):
        far, role, digit = i // 16, lax.rem(i // 8, 2), lax.rem(i, 8)
        half = jnp.where(far == 0, 1 - z, z)
        rows = pl.ds(pl.multiple_of(half * 128, 128), 128)
        lanes = pl.ds(pl.multiple_of(digit * N + role * HALF, 128), 128)
        slot = lax.rem(i, SLOTS)
        return pltpu.make_async_copy(
            transfer.at[:, :, rows, lanes], slabs.at[slot], slab_sem.at[slot]
        )

    consts = [
        pltpu.make_async_copy(amplitudes, amp, const_sem.at[0]),
        pltpu.make_async_copy(order, order_v, const_sem.at[1]),
        pltpu.make_async_copy(first, first_v, const_sem.at[2]),
        pltpu.make_async_copy(twist.at[me], twist_v, const_sem.at[3]),
    ]
    consts[0].start()

    @pl.loop(0, SLOTS)
    def _(i):
        slab_copy(i).start()

    consts[1].start()
    barrier = pltpu.get_barrier_semaphore()
    pl.semaphore_signal(barrier, inc=1, device_id=other_z, device_id_type=MESH)
    pl.semaphore_signal(barrier, inc=1, device_id=other_core, device_id_type=MESH)
    for to in others:
        pl.semaphore_signal(barrier, inc=1, device_id=(head, to), device_id_type=MESH)

    consts[0].wait()
    for r in range(2):
        for h in range(HEADS):
            row = amp[h, r : r + 1, :] * weights[h]
            wide[r, h] = jnp.broadcast_to(row, (8, row.shape[1]))

    def add_headings(chunk):
        @pl.loop(0, 4)
        def _(s):
            i = chunk * 4 + s
            role, digit = lax.rem(i // 8, 2), lax.rem(i, 8)
            lanes = pl.ds(pl.multiple_of(digit * N + role * HALF, 128), 128)
            slot = lax.rem(i, SLOTS)
            slab_copy(i).wait()

            @pl.loop(0, 2)
            def _(mine):
                row = jnp.where(mine == 0, 1 - core, core) * SPOTS
                for tile in range(SPOTS // 16):
                    rows = pl.ds(pl.multiple_of(row + tile * 16, 16), 16)
                    real = imag = None
                    for h in range(HEADS):
                        tr = slabs[slot, 0, h, rows, :].astype(f32).reshape(2, 8, 128)
                        ti = slabs[slot, 1, h, rows, :].astype(f32).reshape(2, 8, 128)
                        wr = wide[0, h, :, lanes][None]
                        wi = wide[1, h, :, lanes][None]
                        re, im = tr * wr - ti * wi, tr * wi + ti * wr
                        real = re if real is None else real + re
                        imag = im if imag is None else imag + im
                    part[mine, chunk, s, tile * 16 : tile * 16 + 16, :] = real.reshape(16, 128)
                    part[mine, chunk, s, SPOTS + tile * 16 : SPOTS + tile * 16 + 16, :] = (
                        imag.reshape(16, 128)
                    )

            @pl.when(i + SLOTS < 32)
            def _():
                slab_copy(i + SLOTS).start()

    def core_copy(chunk):
        return pltpu.make_async_remote_copy(
            src_ref=part.at[0, chunk], dst_ref=core_in.at[chunk],
            send_sem=core_send.at[chunk], recv_sem=core_recv.at[chunk],
            device_id=other_core, device_id_type=MESH,
        )

    def pair_copy(chunk):
        return pltpu.make_async_remote_copy(
            src_ref=pair_out.at[chunk], dst_ref=pair_in.at[chunk],
            send_sem=pair_send.at[chunk], recv_sem=pair_recv.at[chunk],
            device_id=other_z, device_id_type=MESH,
        )

    def to_rows(table, value):
        return lax.dot_general(
            table, value, (((1,), (1,)), ((), ())), preferred_element_type=f32
        )

    def place(chunk, s, pairs):
        role, digit = chunk % 4 // 2, chunk % 2 * 4 + s
        return pl.ds(role * AL + digit, FREQ * pairs, stride=2 * AL)

    def chip_sum(chunk):
        core_copy(chunk).wait_recv()
        return (part[1, chunk] + core_in[chunk]).reshape(4 * 128, 128)

    def move_far(chunk):
        moved = to_rows(order_v[chunk // 2], chip_sum(chunk).astype(bf16))
        for s in range(4):
            slab = moved[:, s * 128 : s * 128 + 128]
            pair_out[chunk, s] = slab[: FREQ * EARLY].astype(bf16)
            gather_late[0, place(chunk, s, LATE), :] = slab[FREQ * EARLY :]
        pair_copy(chunk).start()

    def move_own(chunk):
        value = chip_sum(chunk)
        upper = value.astype(bf16)
        lower = (value - upper.astype(f32)).astype(bf16)
        role = (chunk - 4) // 2
        moved = to_rows(order_v[role], upper)
        rest = to_rows(order_v[role, : FREQ * EARLY], lower)
        for s in range(4):
            lanes = slice(s * 128, s * 128 + 128)
            early_own[chunk - 4, s] = moved[: FREQ * EARLY, lanes] + rest[:, lanes]
            gather_late[1, place(chunk, s, LATE), :] = moved[FREQ * EARLY :, lanes]

    def send_all(source, landing, send_sem, recv_sem):
        for to in others:
            pltpu.make_async_remote_copy(
                src_ref=source.at[to], dst_ref=landing.at[me],
                send_sem=send_sem, recv_sem=recv_sem,
                device_id=(head, to), device_id_type=MESH,
            ).start()
        landing[me] = source[me]

    def all_but_one(ref, sem):
        return pltpu.make_async_copy(ref.at[pl.ds(0, FREQ - 1)], ref.at[pl.ds(0, FREQ - 1)], sem)

    def send_late(group):
        late_out[group] = gather_late[group].reshape(FREQ, LATE * 2 * AL, 128).astype(bf16)
        send_all(late_out.at[group], late_in.at[group], bins_send.at[group], bins_recv.at[group])

    for chunk in range(8):
        add_headings(chunk)
        if chunk == 0:
            pl.semaphore_wait(barrier, FREQ + 1)
            consts[1].wait()
        core_copy(chunk).start()
        if 1 <= chunk <= 4:
            move_far(chunk - 1)
        if chunk == 4:
            send_late(0)
            for c in consts[2:]:
                c.start()
        if chunk > 4:
            move_own(chunk - 1)
    move_own(7)
    send_late(1)
    for c in consts[2:]:
        c.wait()
    for i in range(4 * PL):
        turn[i] = jnp.broadcast_to(twist_v[:, i : i + 1], (N, 128))

    for chunk in range(4):
        pair_copy(chunk).wait_recv()
        for s in range(4):
            gather_early[place(chunk, s, EARLY), :] = (
                early_own[chunk, s] + pair_in[chunk, s].astype(f32)
            )
    early_out[...] = gather_early[...].reshape(FREQ, EARLY * 2 * AL, 128).astype(bf16)
    send_all(early_out, early_in, bins_send.at[2], bins_recv.at[2])

    lane = lax.broadcasted_iota(jnp.int32, (1, 128), 1)
    low = lane < SPOTS
    sign = jnp.where(low, -1.0, 1.0).astype(f32)
    lone = jnp.where(me == 0, 0.0, 1.0).astype(f32)
    ones = jnp.ones((1, 128), f32)

    def first_pass(bins, pairs, store):
        count = len(pairs)
        both = jnp.concatenate(
            [bins[:, i * 16 : i * 16 + 16, :].reshape(2 * N, 128) for i in range(count)], axis=1
        )
        for role in range(2):
            passed[role, :, : count * 128] = jnp.dot(
                first_v[role * 2 * N : (role + 1) * 2 * N, :], both, preferred_element_type=f32
            )
        for i, p in enumerate(pairs):
            if p == 0:
                a, b = jnp.where(low, ones, lone), jnp.where(low, lone, -ones)
                a_far, b_far = jnp.where(low, lone, ones), jnp.where(low, -ones, lone)
            else:
                a, b, a_far, b_far = ones, -sign, ones, sign

            @pl.loop(0, 4)
            def _(block):
                rows = pl.ds(pl.multiple_of(block * 64, 64), 64)
                more = pl.ds(pl.multiple_of(N + block * 64, 64), 64)
                lanes = slice(i * 128, i * 128 + 128)
                straight, crossed = [], []
                for role in range(2):
                    c, s = passed[role, rows, lanes], passed[role, more, lanes]
                    column = (role * PL + p) * 2
                    cw, sw = turn[column, rows, :], turn[column + 1, rows, :]
                    straight.append(c * cw - s * sw)
                    crossed.append(s * cw + c * sw)
                value = a * straight[0] + b * straight[1]
                value += sign * pltpu.roll(a_far * crossed[0] + b_far * crossed[1], SPOTS, 1)
                store(i, pl.ds(pl.multiple_of(block * 8, 8), 8), value.reshape(8, AL, 128))

    def store_cross(i, times, value):
        late_folded[times, i * AL : i * AL + AL, :] = value

    def store_late(i, times, value):
        folded[times, (EARLY + i) * AL : (EARLY + i + 1) * AL, :] = value

    def store_early(i, times, value):
        folded[times, i * AL : i * AL + AL, :] = value

    late_pairs = list(range(EARLY, PL))
    all_but_one(late_in.at[0], bins_recv.at[0]).wait()
    first_pass(late_in.at[0], late_pairs, store_cross)
    cross_out[...] = late_folded[...].astype(bf16)
    cross = pltpu.make_async_remote_copy(
        src_ref=cross_out, dst_ref=cross_in, send_sem=cross_send.at[0],
        recv_sem=cross_recv.at[0], device_id=other_z, device_id_type=MESH,
    )
    cross.start()
    all_but_one(late_in.at[1], bins_recv.at[1]).wait()
    first_pass(late_in.at[1], late_pairs, store_late)
    all_but_one(early_in, bins_recv.at[2]).wait()
    first_pass(early_in, list(range(EARLY)), store_early)

    cross.wait_recv()
    fold_out[:, : EARLY * AL, :] = folded[:, : EARLY * AL, :].astype(bf16)
    fold_out[:, EARLY * AL :, :] = (
        folded[:, EARLY * AL :, :] + cross_in[...].astype(f32)
    ).astype(bf16)
    send_all(fold_out, fold_in, fold_send.at[0], fold_recv.at[0])

    for chunk in range(8):
        core_copy(chunk).wait_send()
    for chunk in range(4):
        pair_copy(chunk).wait_send()
    cross.wait_send()
    for group in range(2):
        all_but_one(late_out.at[group], bins_send.at[group]).wait()
    all_but_one(early_out, bins_send.at[2]).wait()
    all_but_one(fold_in, fold_recv.at[0]).wait()
    out[...] = fold_in[...]
    all_but_one(fold_out, fold_send.at[0]).wait()


def second_kernel(fold_in, second_v, out, fold_f32, staged):
    f32, bf16 = jnp.float32, jnp.bfloat16
    fold_f32[...] = fold_in[...].astype(f32).reshape(FREQ * PL * AL, 128)
    for t in range(AL):
        value = fold_f32[pl.ds(t, HALF, stride=AL), :].astype(bf16)
        value = jnp.concatenate([value, value], axis=0)
        result = lax.dot_general(
            value, second_v[...], (((0,), (0,)), ((), ())), preferred_element_type=f32
        )
        result = result[:SPOTS, :N] + result[SPOTS:, N:]
        for i in range(2):
            staged[i, pl.ds(t, SPOTS, stride=AL), :] = result[:, i * 128 : i * 128 + 128]
    for i in range(2):
        out[:, i * 128 : i * 128 + 128] = staged[i]


def on_device(transfer, amplitudes, weights):
    f32, bf16 = jnp.float32, jnp.bfloat16
    any_spec = pl.BlockSpec(memory_space=pl.ANY)
    first, order, twist, second = [jnp.asarray(table) for table in tables()]
    folded = pl.pallas_call(
        kernel,
        out_shape=jax.ShapeDtypeStruct((FREQ, PL * AL, 128), bf16),
        in_specs=[any_spec, any_spec, pl.BlockSpec(memory_space=pltpu.SMEM)] + [any_spec] * 3,
        out_specs=pl.BlockSpec(memory_space=pltpu.VMEM),
        scratch_shapes=[
            pltpu.VMEM((SLOTS, 2, HEADS, 128, 128), bf16),
            pltpu.VMEM((HEADS, 2, AL * N), f32),
            pltpu.VMEM((2, HEADS, 8, AL * N), f32),
            pltpu.VMEM((2, 8, 4, 128, 128), f32),
            pltpu.VMEM((8, 4, 128, 128), f32),
            pltpu.VMEM((4, 4, FREQ * EARLY, 128), bf16),
            pltpu.VMEM((4, 4, FREQ * EARLY, 128), bf16),
            pltpu.VMEM((4, 4, FREQ * EARLY, 128), f32),
            pltpu.VMEM((FREQ * EARLY * 2 * AL, 128), f32),
            pltpu.VMEM((2, FREQ * LATE * 2 * AL, 128), f32),
            pltpu.VMEM((FREQ, EARLY * 2 * AL, 128), bf16),
            pltpu.VMEM((FREQ, EARLY * 2 * AL, 128), bf16),
            pltpu.VMEM((2, FREQ, LATE * 2 * AL, 128), bf16),
            pltpu.VMEM((2, FREQ, LATE * 2 * AL, 128), bf16),
            pltpu.VMEM((4 * N, 2 * N), bf16),
            pltpu.VMEM((2, HALF, HALF), bf16),
            pltpu.VMEM((N, 128), f32),
            pltpu.VMEM((4 * PL, N, 128), f32),
            pltpu.VMEM((2, 2 * N, max(EARLY, LATE) * 128), f32),
            pltpu.VMEM((FREQ, PL * AL, 128), f32),
            pltpu.VMEM((FREQ, LATE * AL, 128), f32),
            pltpu.VMEM((FREQ, LATE * AL, 128), bf16),
            pltpu.VMEM((FREQ, LATE * AL, 128), bf16),
            pltpu.VMEM((FREQ, PL * AL, 128), bf16),
            pltpu.VMEM((FREQ, PL * AL, 128), bf16),
            pltpu.SemaphoreType.DMA((SLOTS,)),
            pltpu.SemaphoreType.DMA((4,)),
            pltpu.SemaphoreType.DMA((8,)),
            pltpu.SemaphoreType.DMA((8,)),
            pltpu.SemaphoreType.DMA((4,)),
            pltpu.SemaphoreType.DMA((4,)),
            pltpu.SemaphoreType.DMA((3,)),
            pltpu.SemaphoreType.DMA((3,)),
            pltpu.SemaphoreType.DMA((1,)),
            pltpu.SemaphoreType.DMA((1,)),
            pltpu.SemaphoreType.DMA((1,)),
            pltpu.SemaphoreType.DMA((1,)),
        ],
        compiler_params=pltpu.CompilerParams(
            collective_id=0, has_side_effects=True, vmem_limit_bytes=56 * 2**20
        ),
        cost_estimate=pl.CostEstimate(
            flops=900_000_000, bytes_accessed=22_000_000, transcendentals=0
        ),
    )(transfer, jnp.transpose(amplitudes, (1, 0, 2)), weights, first, order, twist)
    stress = pl.pallas_call(
        second_kernel,
        out_shape=jax.ShapeDtypeStruct((SPOTS * AL, N), f32),
        in_specs=[pl.BlockSpec(memory_space=pltpu.VMEM)] * 2,
        out_specs=pl.BlockSpec(memory_space=pltpu.VMEM),
        scratch_shapes=[
            pltpu.VMEM((FREQ * PL * AL, 128), f32),
            pltpu.VMEM((2, SPOTS * AL, 128), f32),
        ],
        cost_estimate=pl.CostEstimate(
            flops=270_000_000, bytes_accessed=1_000_000, transcendentals=0
        ),
    )(folded, second)
    return stress.reshape(SPOTS, AL, N)


def solution(mesh):
    in_specs = (P(None, "head", None, "freq"), P(None, "head", "freq"), P("head"))
    out_specs = P("head", "freq", None)
    return jax.shard_map(
        on_device, mesh=mesh, in_specs=in_specs, out_specs=out_specs, check_vma=False
    )
```

```python
import functools
import math

import jax
import jax.numpy as jnp
import ml_dtypes
import numpy as np
from jax import lax
from jax.experimental import pallas as pl
from jax.experimental.pallas import tpu as pltpu
from jax.sharding import PartitionSpec as P

N = 256
HALF = N // 2
HEADS = 9
SPOTS = 64
FREQ = 32
AL = 8
PL = 4
EARLY = 2
LATE = PL - EARLY
SLOTS = 8
MESH = pl.DeviceIdType.MESH


def tables():
    n = np.arange(N)
    angle = 2.0 * math.pi * ((n[:, None] * n[None, :]) % N) / N
    trig = np.stack([np.cos(angle), np.sin(angle)])
    trig = trig.reshape(2, N, FREQ, AL)
    first = np.zeros((2, 2, N, FREQ, 2, AL))
    for i in range(2):
        first[i, :, :, :, i, :] = trig
    first = first.reshape(4 * N, 2 * N).astype(ml_dtypes.bfloat16)
    pairs = HALF // PL * np.arange(PL) + np.arange(FREQ)[:, None]
    order = np.zeros((2, HALF, HALF))
    order[0] = np.eye(HALF)
    order[1][np.arange(HALF), (HALF - np.arange(HALF)) % HALF] = 1.0
    order = order.astype(ml_dtypes.bfloat16)
    pairs = pairs.reshape(-1)
    mirror = np.where(pairs == 0, HALF, N - pairs)
    low = np.stack([pairs, mirror])
    turn = 2.0 * math.pi * ((low[:, :, None] * n) % (N * N)) / (N * N)
    cos_turn, sin_turn = np.cos(turn), np.sin(turn)
    cos_turn[1, 0], sin_turn[1, 0] = -np.sin(turn[1, 0]), np.cos(turn[1, 0])
    twist = np.stack([cos_turn, sin_turn], axis=2)
    twist = twist.reshape(2, FREQ, PL, 2, N).transpose(1, 4, 0, 2, 3).reshape(FREQ, N, 4 * PL)
    wide = np.zeros((FREQ, N, 128), np.float32)
    wide[:, :, : 4 * PL] = twist
    cos_two, sin_two = np.cos(angle)[:HALF], -np.sin(angle)[:HALF]
    sin_two[0] = -((-1.0) ** n)
    second = np.concatenate([cos_two, sin_two], axis=1).astype(np.float32)[pairs]
    upper = second.astype(ml_dtypes.bfloat16)
    lower = (second - upper.astype(np.float32)).astype(ml_dtypes.bfloat16)
    second = np.concatenate([upper, lower], axis=0)
    return first, order, wide, second


def farthest_first():
    steps = [(y, x, z) for y in range(4) for x in range(4) for z in range(2)]
    return sorted(steps, key=lambda d: -(min(d[0], 4 - d[0]) + min(d[1], 4 - d[1]) + d[2]))[:-1]


def kernel(
    transfer, amplitudes, weights, first, order, twist,
    fold_in,
    slabs, amp, wide, part, core_in, pair_out, pair_in, gather_own, gather_late,
    own_out, own_in, late_out, late_in,
    first_v, order_v, twist_v, turn, passed, folded, cross_out, cross_in,
    fold_out,
    slab_sem, const_sem, core_send, core_recv, pair_send, pair_recv,
    bins_send, bins_recv, cross_send, cross_recv, fold_send, fold_recv,
):
    head = lax.axis_index("head")
    me = lax.axis_index("freq")
    z, core = head // 2, lax.rem(head, 2)
    other_core = (z * 2 + 1 - core, me)
    other_z = ((1 - z) * 2 + core, me)
    f32, bf16 = jnp.float32, jnp.bfloat16
    y, x, z_low = me // 8, lax.rem(me // 2, 4), lax.rem(me, 2)
    others = [
        lax.rem(y + dy, 4) * 8 + lax.rem(x + dx, 4) * 2 + lax.rem(z_low + dz, 2)
        for dy, dx, dz in farthest_first()
    ]

    def slab_copy(i):
        far, role, digit = i // 16, lax.rem(i // 8, 2), lax.rem(i, 8)
        half = jnp.where(far == 0, 1 - z, z)
        rows = pl.ds(pl.multiple_of(half * 128, 128), 128)
        lanes = pl.ds(pl.multiple_of(digit * N + role * HALF, 128), 128)
        slot = lax.rem(i, SLOTS)
        return pltpu.make_async_copy(
            transfer.at[:, :, rows, lanes], slabs.at[slot], slab_sem.at[slot]
        )

    consts = [
        pltpu.make_async_copy(amplitudes, amp, const_sem.at[0]),
        pltpu.make_async_copy(order, order_v, const_sem.at[1]),
        pltpu.make_async_copy(first, first_v, const_sem.at[2]),
        pltpu.make_async_copy(twist.at[me], twist_v, const_sem.at[3]),
    ]
    consts[0].start()

    @pl.loop(0, SLOTS)
    def _(i):
        slab_copy(i).start()

    consts[1].start()
    barrier = pltpu.get_barrier_semaphore()
    pl.semaphore_signal(barrier, inc=1, device_id=other_z, device_id_type=MESH)
    pl.semaphore_signal(barrier, inc=1, device_id=other_core, device_id_type=MESH)
    for to in others:
        pl.semaphore_signal(barrier, inc=1, device_id=(head, to), device_id_type=MESH)

    consts[0].wait()
    for r in range(2):
        for h in range(HEADS):
            row = amp[h, r : r + 1, :] * weights[h]
            wide[r, h] = jnp.broadcast_to(row, (8, row.shape[1]))

    def add_headings(chunk):
        @pl.loop(0, 4)
        def _(s):
            i = chunk * 4 + s
            role, digit = lax.rem(i // 8, 2), lax.rem(i, 8)
            lanes = pl.ds(pl.multiple_of(digit * N + role * HALF, 128), 128)
            slot = lax.rem(i, SLOTS)
            slab_copy(i).wait()

            @pl.loop(0, 2)
            def _(mine):
                row = jnp.where(mine == 0, 1 - core, core) * SPOTS
                for first_tile in range(0, SPOTS // 16, 4):
                    tiles = range(first_tile, first_tile + 4)
                    sums = [[None, None] for _ in tiles]
                    for h in range(HEADS):
                        wr, wi = wide[0, h, :, lanes][None], wide[1, h, :, lanes][None]
                        for k, tile in enumerate(tiles):
                            rows = pl.ds(pl.multiple_of(row + tile * 16, 16), 16)
                            tr = slabs[slot, 0, h, rows, :].astype(f32).reshape(2, 8, 128)
                            ti = slabs[slot, 1, h, rows, :].astype(f32).reshape(2, 8, 128)
                            re, im = tr * wr - ti * wi, tr * wi + ti * wr
                            sums[k] = [re, im] if h == 0 else [sums[k][0] + re, sums[k][1] + im]
                    for k, tile in enumerate(tiles):
                        for c in range(2):
                            part[mine, chunk, s, pl.ds(c * SPOTS + tile * 16, 16), :] = (
                                sums[k][c].reshape(16, 128)
                            )

            @pl.when(i + SLOTS < 32)
            def _():
                slab_copy(i + SLOTS).start()

    def core_copy(chunk):
        return pltpu.make_async_remote_copy(
            src_ref=part.at[0, chunk], dst_ref=core_in.at[chunk],
            send_sem=core_send.at[chunk], recv_sem=core_recv.at[chunk],
            device_id=other_core, device_id_type=MESH,
        )

    def pair_copy(chunk):
        return pltpu.make_async_remote_copy(
            src_ref=pair_out.at[chunk], dst_ref=pair_in.at[chunk],
            send_sem=pair_send.at[chunk], recv_sem=pair_recv.at[chunk],
            device_id=other_z, device_id_type=MESH,
        )

    def to_rows(table, value):
        return lax.dot_general(
            table, value, (((1,), (1,)), ((), ())), preferred_element_type=f32
        )

    def digit_of(chunk, s):
        return chunk % 2 * 4 + s

    def chip_sum(chunk):
        core_copy(chunk).wait_recv()
        return (part[1, chunk] + core_in[chunk]).reshape(4 * 128, 128)

    def move_far(chunk):
        role = chunk // 2
        moved = to_rows(order_v[role], chip_sum(chunk).astype(bf16))
        for s in range(4):
            slab = moved[:, s * 128 : s * 128 + 128]
            pair_out[chunk, s] = slab[: FREQ * EARLY].astype(bf16)
            for i in range(LATE):
                row = i * 2 * AL + role * AL + digit_of(chunk, s)
                gather_late[pl.ds(row, FREQ, stride=LATE * 2 * AL), :] = slab[
                    FREQ * (EARLY + i) : FREQ * (EARLY + i + 1)
                ]
        pair_copy(chunk).start()

    def move_own(chunk):
        value = chip_sum(4 + chunk)
        upper = value.astype(bf16)
        lower = (value - upper.astype(f32)).astype(bf16)
        role = chunk // 2
        moved = to_rows(order_v[role], upper)
        rest = to_rows(order_v[role, : FREQ * EARLY], lower)
        pair_copy(chunk).wait_recv()
        for s in range(4):
            lanes = slice(s * 128, s * 128 + 128)
            full = moved[: FREQ * EARLY, lanes] + rest[:, lanes] + pair_in[chunk, s].astype(f32)
            for i in range(PL):
                rows = slice(FREQ * i, FREQ * (i + 1))
                gather_own[
                    role, pl.ds(i * AL + digit_of(chunk, s), FREQ, stride=PL * AL), :
                ] = full[rows] if i < EARLY else moved[rows, lanes]

    def send_all(source, landing, send_sem, recv_sem):
        for to in others:
            pltpu.make_async_remote_copy(
                src_ref=source.at[to], dst_ref=landing.at[me],
                send_sem=send_sem, recv_sem=recv_sem,
                device_id=(head, to), device_id_type=MESH,
            ).start()
        landing[me] = source[me]

    def all_but_one(ref, sem):
        return pltpu.make_async_copy(ref.at[pl.ds(0, FREQ - 1)], ref.at[pl.ds(0, FREQ - 1)], sem)

    def send_late():
        late_out[...] = gather_late[...].reshape(FREQ, LATE * 2 * AL, 128).astype(bf16)
        send_all(late_out, late_in, bins_send.at[2], bins_recv.at[2])

    def send_own(role):
        own_out[role] = gather_own[role].reshape(FREQ, PL * AL, 128).astype(bf16)
        send_all(own_out.at[role], own_in.at[role], bins_send.at[role], bins_recv.at[role])

    for chunk in range(8):
        add_headings(chunk)
        if chunk == 0:
            pl.semaphore_wait(barrier, FREQ + 1)
            consts[1].wait()
        core_copy(chunk).start()
        if 1 <= chunk <= 4:
            move_far(chunk - 1)
        if chunk == 4:
            send_late()
            for c in consts[2:]:
                c.start()
        if chunk > 4:
            move_own(chunk - 5)
    send_own(0)
    move_own(3)
    send_own(1)
    for c in consts[2:]:
        c.wait()
    for i in range(4 * PL):
        turn[i] = jnp.broadcast_to(twist_v[:, i : i + 1], (N, 128))

    lane = lax.broadcasted_iota(jnp.int32, (1, 128), 1)
    low = lane < SPOTS
    sign = jnp.where(low, -1.0, 1.0).astype(f32)
    lone = jnp.where(me == 0, 0.0, 1.0).astype(f32)
    ones = jnp.ones((1, 128), f32)

    def masks(p):
        if p > 0:
            return ones, -sign, ones, sign
        return (
            jnp.where(low, ones, lone), jnp.where(low, lone, -ones),
            jnp.where(low, lone, ones), jnp.where(low, -ones, lone),
        )

    def first_pass(bins, count):
        both = jnp.concatenate(
            [bins[:, i * 16 : i * 16 + 16, :].reshape(2 * N, 128) for i in range(count)], axis=1
        )
        for stream in range(2):
            passed[stream, :, : count * 128] = jnp.dot(
                first_v[stream * 2 * N : (stream + 1) * 2 * N, :], both, preferred_element_type=f32
            )

    def twisted(stream, place, block, role, p):
        rows = pl.ds(pl.multiple_of(block * 64, 64), 64)
        more = pl.ds(pl.multiple_of(N + block * 64, 64), 64)
        lanes = slice(place * 128, place * 128 + 128)
        c, s = passed[stream, rows, lanes], passed[stream, more, lanes]
        column = (role * PL + p) * 2
        cw, sw = turn[column, rows, :], turn[column + 1, rows, :]
        return c * cw - s * sw, s * cw + c * sw

    def swap(value):
        return sign * pltpu.roll(value, SPOTS, 1)

    all_but_one(late_in, bins_recv.at[2]).wait()
    first_pass(late_in, LATE)

    @pl.loop(0, 4)
    def _(block):
        values = []
        for i in range(LATE):
            a, b, a_far, b_far = masks(EARLY + i)
            straight, crossed = twisted(0, i, block, 0, EARLY + i)
            straight_far, crossed_far = twisted(1, i, block, 1, EARLY + i)
            value = a * straight + b * straight_far + swap(a_far * crossed + b_far * crossed_far)
            values.append(value.reshape(8, AL, 128))
        times = pl.ds(pl.multiple_of(block * 8, 8), 8)
        cross_out[times] = jnp.concatenate(values, axis=1).astype(bf16)

    cross = pltpu.make_async_remote_copy(
        src_ref=cross_out, dst_ref=cross_in, send_sem=cross_send.at[0],
        recv_sem=cross_recv.at[0], device_id=other_z, device_id_type=MESH,
    )
    cross.start()

    for role in range(2):
        all_but_one(own_in.at[role], bins_recv.at[role]).wait()
        first_pass(own_in.at[role], 2)
        for place in range(2):
            if role == 1 and place == 1:
                cross.wait_recv()

            @pl.loop(0, 4)
            def _(block):
                values = []
                for stream in range(2):
                    p = place * 2 + stream
                    straight, crossed = twisted(stream, place, block, role, p)
                    values.append((masks(p)[role] * straight + swap(masks(p)[2 + role] * crossed)).reshape(8, AL, 128))
                value = jnp.concatenate(values, axis=1)
                times = pl.ds(pl.multiple_of(block * 8, 8), 8)
                rows = slice(place * 16, place * 16 + 16)
                if role == 0:
                    folded[times, rows, :] = value
                else:
                    value += folded[times, rows, :]
                    if place == 1:
                        value += cross_in[times].astype(f32)
                    fold_out[times, rows, :] = value.astype(bf16)

    send_all(fold_out, fold_in, fold_send.at[0], fold_recv.at[0])

    for chunk in range(8):
        core_copy(chunk).wait_send()
    for chunk in range(4):
        pair_copy(chunk).wait_send()
    cross.wait_send()
    for role in range(2):
        all_but_one(own_out.at[role], bins_send.at[role]).wait()
    all_but_one(late_out, bins_send.at[2]).wait()
    all_but_one(fold_in, fold_recv.at[0]).wait()
    all_but_one(fold_out, fold_send.at[0]).wait()


def second_kernel(fold_in, second_v, out, fold_f32, staged):
    f32, bf16 = jnp.float32, jnp.bfloat16
    fold_f32[...] = fold_in[...].astype(f32).reshape(FREQ * PL * AL, 128)
    for t in range(AL):
        value = fold_f32[pl.ds(t, HALF, stride=AL), :].astype(bf16)
        value = jnp.concatenate([value, value], axis=0)
        result = lax.dot_general(
            value, second_v[...], (((0,), (0,)), ((), ())), preferred_element_type=f32
        )
        result = result[:SPOTS, :N] + result[SPOTS:, N:]
        for i in range(2):
            staged[i, pl.ds(t, SPOTS, stride=AL), :] = result[:, i * 128 : i * 128 + 128]
    for i in range(2):
        out[:, i * 128 : i * 128 + 128] = staged[i]


def on_device(transfer, amplitudes, weights):
    f32, bf16 = jnp.float32, jnp.bfloat16
    any_spec = pl.BlockSpec(memory_space=pl.ANY)
    first, order, twist, second = [jnp.asarray(table) for table in tables()]
    folded = pl.pallas_call(
        kernel,
        out_shape=pltpu.VMEM((FREQ, PL * AL, 128), bf16),
        in_specs=[any_spec, any_spec, pl.BlockSpec(memory_space=pltpu.SMEM)] + [any_spec] * 3,
        out_specs=pl.BlockSpec(memory_space=pltpu.VMEM),
        scratch_shapes=[
            pltpu.VMEM((SLOTS, 2, HEADS, 128, 128), bf16),
            pltpu.VMEM((HEADS, 2, AL * N), f32),
            pltpu.VMEM((2, HEADS, 8, AL * N), f32),
            pltpu.VMEM((2, 8, 4, 128, 128), f32),
            pltpu.VMEM((8, 4, 128, 128), f32),
            pltpu.VMEM((4, 4, FREQ * EARLY, 128), bf16),
            pltpu.VMEM((4, 4, FREQ * EARLY, 128), bf16),
            pltpu.VMEM((2, FREQ * PL * AL, 128), f32),
            pltpu.VMEM((FREQ * LATE * 2 * AL, 128), f32),
            pltpu.VMEM((2, FREQ, PL * AL, 128), bf16),
            pltpu.VMEM((2, FREQ, PL * AL, 128), bf16),
            pltpu.VMEM((FREQ, LATE * 2 * AL, 128), bf16),
            pltpu.VMEM((FREQ, LATE * 2 * AL, 128), bf16),
            pltpu.VMEM((4 * N, 2 * N), bf16),
            pltpu.VMEM((2, HALF, HALF), bf16),
            pltpu.VMEM((N, 128), f32),
            pltpu.VMEM((4 * PL, N, 128), f32),
            pltpu.VMEM((2, 2 * N, 2 * 128), f32),
            pltpu.VMEM((FREQ, PL * AL, 128), f32),
            pltpu.VMEM((FREQ, LATE * AL, 128), bf16),
            pltpu.VMEM((FREQ, LATE * AL, 128), bf16),
            pltpu.VMEM((FREQ, PL * AL, 128), bf16),
            pltpu.SemaphoreType.DMA((SLOTS,)),
            pltpu.SemaphoreType.DMA((4,)),
            pltpu.SemaphoreType.DMA((8,)),
            pltpu.SemaphoreType.DMA((8,)),
            pltpu.SemaphoreType.DMA((4,)),
            pltpu.SemaphoreType.DMA((4,)),
            pltpu.SemaphoreType.DMA((3,)),
            pltpu.SemaphoreType.DMA((3,)),
            pltpu.SemaphoreType.DMA((1,)),
            pltpu.SemaphoreType.DMA((1,)),
            pltpu.SemaphoreType.DMA((1,)),
            pltpu.SemaphoreType.DMA((1,)),
        ],
        compiler_params=pltpu.CompilerParams(
            collective_id=0, has_side_effects=True, vmem_limit_bytes=56 * 2**20
        ),
        cost_estimate=pl.CostEstimate(
            flops=900_000_000, bytes_accessed=22_000_000, transcendentals=0
        ),
    )(transfer, jnp.transpose(amplitudes, (1, 0, 2)), weights, first, order, twist)
    stress = pl.pallas_call(
        second_kernel,
        out_shape=jax.ShapeDtypeStruct((SPOTS * AL, N), f32),
        in_specs=[pl.BlockSpec(memory_space=pltpu.VMEM)] * 2,
        out_specs=pl.BlockSpec(memory_space=pltpu.VMEM),
        scratch_shapes=[
            pltpu.VMEM((FREQ * PL * AL, 128), f32),
            pltpu.VMEM((2, SPOTS * AL, 128), f32),
        ],
        cost_estimate=pl.CostEstimate(
            flops=270_000_000, bytes_accessed=1_000_000, transcendentals=0
        ),
    )(pltpu.with_memory_space_constraint(folded, pltpu.VMEM), second)
    return stress.reshape(SPOTS, AL, N)


def solution(mesh):
    in_specs = (P(None, "head", None, "freq"), P(None, "head", "freq"), P("head"))
    out_specs = P("head", "freq", None)
    return jax.shard_map(
        on_device, mesh=mesh, in_specs=in_specs, out_specs=out_specs, check_vma=False
    )
```

```python
import functools
import math

import jax
import jax.numpy as jnp
import ml_dtypes
import numpy as np
from jax import lax
from jax.experimental import pallas as pl
from jax.experimental.pallas import tpu as pltpu
from jax.sharding import PartitionSpec as P

N = 256
HALF = N // 2
HEADS = 9
SPOTS = 64
FREQ = 32
AL = 8
PL = 4
EARLY = 2
LATE = PL - EARLY
SLOTS = 8
MESH = pl.DeviceIdType.MESH


def tables():
    n = np.arange(N)
    angle = 2.0 * math.pi * ((n[:, None] * n[None, :]) % N) / N
    trig = np.stack([np.cos(angle), np.sin(angle)])
    trig = trig.reshape(2, N, FREQ, AL)
    first = np.zeros((2, 2, N, FREQ, 2, AL))
    for i in range(2):
        first[i, :, :, :, i, :] = trig
    first = first.reshape(4 * N, 2 * N).astype(ml_dtypes.bfloat16)
    pairs = HALF // PL * np.arange(PL) + np.arange(FREQ)[:, None]
    order = np.zeros((2, HALF, HALF))
    order[0] = np.eye(HALF)
    order[1][np.arange(HALF), (HALF - np.arange(HALF)) % HALF] = 1.0
    order = order.astype(ml_dtypes.bfloat16)
    pairs = pairs.reshape(-1)
    mirror = np.where(pairs == 0, HALF, N - pairs)
    low = np.stack([pairs, mirror])
    turn = 2.0 * math.pi * ((low[:, :, None] * n) % (N * N)) / (N * N)
    cos_turn, sin_turn = np.cos(turn), np.sin(turn)
    cos_turn[1, 0], sin_turn[1, 0] = -np.sin(turn[1, 0]), np.cos(turn[1, 0])
    twist = np.stack([cos_turn, sin_turn], axis=2)
    twist = twist.reshape(2, FREQ, PL, 2, N).transpose(1, 4, 0, 2, 3).reshape(FREQ, N, 4 * PL)
    wide = np.zeros((FREQ, N, 128), np.float32)
    wide[:, :, : 4 * PL] = twist
    cos_two, sin_two = np.cos(angle)[:HALF], -np.sin(angle)[:HALF]
    sin_two[0] = -((-1.0) ** n)
    second = np.concatenate([cos_two, sin_two], axis=1).astype(np.float32)[pairs]
    upper = second.astype(ml_dtypes.bfloat16)
    lower = (second - upper.astype(np.float32)).astype(ml_dtypes.bfloat16)
    second = np.concatenate([upper, lower], axis=0)
    return first, order, wide, second


def farthest_first():
    steps = [(y, x, z) for y in range(4) for x in range(4) for z in range(2)]
    return sorted(steps, key=lambda d: -(min(d[0], 4 - d[0]) + min(d[1], 4 - d[1]) + d[2]))[:-1]


def kernel(
    transfer, amplitudes, weights, first, order, twist, second,
    fold_in, second_v,
    slabs, amp, wide, part, core_in, pair_out, pair_in, gather_own, gather_late,
    own_out, own_in, late_out, late_in,
    first_v, order_v, twist_v, turn, passed, folded, cross_out, cross_in,
    fold_out,
    slab_sem, const_sem, core_send, core_recv, pair_send, pair_recv,
    bins_send, bins_recv, cross_send, cross_recv, fold_send, fold_recv,
):
    head = lax.axis_index("head")
    me = lax.axis_index("freq")
    z, core = head // 2, lax.rem(head, 2)
    other_core = (z * 2 + 1 - core, me)
    other_z = ((1 - z) * 2 + core, me)
    f32, bf16 = jnp.float32, jnp.bfloat16
    y, x, z_low = me // 8, lax.rem(me // 2, 4), lax.rem(me, 2)
    others = [
        lax.rem(y + dy, 4) * 8 + lax.rem(x + dx, 4) * 2 + lax.rem(z_low + dz, 2)
        for dy, dx, dz in farthest_first()
    ]

    def slab_copy(i):
        far, role, digit = i // 16, lax.rem(i // 8, 2), lax.rem(i, 8)
        half = jnp.where(far == 0, 1 - z, z)
        rows = pl.ds(pl.multiple_of(half * 128, 128), 128)
        lanes = pl.ds(pl.multiple_of(digit * N + role * HALF, 128), 128)
        slot = lax.rem(i, SLOTS)
        return pltpu.make_async_copy(
            transfer.at[:, :, rows, lanes], slabs.at[slot], slab_sem.at[slot]
        )

    consts = [
        pltpu.make_async_copy(amplitudes, amp, const_sem.at[0]),
        pltpu.make_async_copy(order, order_v, const_sem.at[1]),
        pltpu.make_async_copy(first, first_v, const_sem.at[2]),
        pltpu.make_async_copy(twist.at[me], twist_v, const_sem.at[3]),
        pltpu.make_async_copy(second, second_v, const_sem.at[4]),
    ]
    consts[0].start()
    consts[3].start()

    @pl.loop(0, SLOTS)
    def _(i):
        slab_copy(i).start()

    consts[1].start()
    barrier = pltpu.get_barrier_semaphore()
    pl.semaphore_signal(barrier, inc=1, device_id=other_z, device_id_type=MESH)
    pl.semaphore_signal(barrier, inc=1, device_id=other_core, device_id_type=MESH)
    for to in others:
        pl.semaphore_signal(barrier, inc=1, device_id=(head, to), device_id_type=MESH)

    consts[0].wait()
    for r in range(2):
        for h in range(HEADS):
            row = amp[h, r : r + 1, :] * weights[h]
            wide[r, h] = jnp.broadcast_to(row, (8, row.shape[1]))

    consts[3].wait()
    for i in range(4 * PL):
        turn[i] = jnp.broadcast_to(twist_v[:, i : i + 1], (N, 128))

    def add_headings(chunk):
        @pl.loop(0, 4)
        def _(s):
            i = chunk * 4 + s
            role, digit = lax.rem(i // 8, 2), lax.rem(i, 8)
            lanes = pl.ds(pl.multiple_of(digit * N + role * HALF, 128), 128)
            slot = lax.rem(i, SLOTS)
            slab_copy(i).wait()

            @pl.loop(0, 2)
            def _(mine):
                row = jnp.where(mine == 0, 1 - core, core) * SPOTS
                for first_tile in range(0, SPOTS // 16, 4):
                    tiles = range(first_tile, first_tile + 4)
                    sums = [[None, None] for _ in tiles]
                    for h in range(HEADS):
                        wr, wi = wide[0, h, :, lanes][None], wide[1, h, :, lanes][None]
                        for k, tile in enumerate(tiles):
                            rows = pl.ds(pl.multiple_of(row + tile * 16, 16), 16)
                            tr = slabs[slot, 0, h, rows, :].astype(f32).reshape(2, 8, 128)
                            ti = slabs[slot, 1, h, rows, :].astype(f32).reshape(2, 8, 128)
                            re, im = tr * wr - ti * wi, tr * wi + ti * wr
                            sums[k] = [re, im] if h == 0 else [sums[k][0] + re, sums[k][1] + im]
                    for k, tile in enumerate(tiles):
                        for c in range(2):
                            part[mine, chunk, s, pl.ds(c * SPOTS + tile * 16, 16), :] = (
                                sums[k][c].reshape(16, 128)
                            )

            @pl.when(i + SLOTS < 32)
            def _():
                slab_copy(i + SLOTS).start()

    def core_copy(chunk):
        return pltpu.make_async_remote_copy(
            src_ref=part.at[0, chunk], dst_ref=core_in.at[chunk],
            send_sem=core_send.at[chunk], recv_sem=core_recv.at[chunk],
            device_id=other_core, device_id_type=MESH,
        )

    def pair_copy(chunk):
        return pltpu.make_async_remote_copy(
            src_ref=pair_out.at[chunk], dst_ref=pair_in.at[chunk],
            send_sem=pair_send.at[chunk], recv_sem=pair_recv.at[chunk],
            device_id=other_z, device_id_type=MESH,
        )

    def to_rows(table, value):
        return lax.dot_general(
            table, value, (((1,), (1,)), ((), ())), preferred_element_type=f32
        )

    def digit_of(chunk, s):
        return chunk % 2 * 4 + s

    def chip_sum(chunk):
        core_copy(chunk).wait_recv()
        return (part[1, chunk] + core_in[chunk]).reshape(4 * 128, 128)

    def move_far(chunk):
        role = chunk // 2
        moved = to_rows(order_v[role], chip_sum(chunk).astype(bf16))
        for s in range(4):
            slab = moved[:, s * 128 : s * 128 + 128]
            pair_out[chunk, s] = slab[: FREQ * EARLY].astype(bf16)
            for i in range(LATE):
                row = i * 2 * AL + role * AL + digit_of(chunk, s)
                gather_late[pl.ds(row, FREQ, stride=LATE * 2 * AL), :] = slab[
                    FREQ * (EARLY + i) : FREQ * (EARLY + i + 1)
                ]
        pair_copy(chunk).start()

    def move_own(chunk):
        value = chip_sum(4 + chunk)
        upper = value.astype(bf16)
        lower = (value - upper.astype(f32)).astype(bf16)
        role = chunk // 2
        moved = to_rows(order_v[role], upper)
        rest = to_rows(order_v[role, : FREQ * EARLY], lower)
        pair_copy(chunk).wait_recv()
        for s in range(4):
            lanes = slice(s * 128, s * 128 + 128)
            full = moved[: FREQ * EARLY, lanes] + rest[:, lanes] + pair_in[chunk, s].astype(f32)
            for i in range(PL):
                rows = slice(FREQ * i, FREQ * (i + 1))
                gather_own[
                    role, pl.ds(i * AL + digit_of(chunk, s), FREQ, stride=PL * AL), :
                ] = full[rows] if i < EARLY else moved[rows, lanes]

    def send_all(source, landing, send_sem, recv_sem):
        for to in others:
            pltpu.make_async_remote_copy(
                src_ref=source.at[to], dst_ref=landing.at[me],
                send_sem=send_sem, recv_sem=recv_sem,
                device_id=(head, to), device_id_type=MESH,
            ).start()
        landing[me] = source[me]

    def all_but_one(ref, sem):
        return pltpu.make_async_copy(ref.at[pl.ds(0, FREQ - 1)], ref.at[pl.ds(0, FREQ - 1)], sem)

    def send_late():
        late_out[...] = gather_late[...].reshape(FREQ, LATE * 2 * AL, 128).astype(bf16)
        send_all(late_out, late_in, bins_send.at[2], bins_recv.at[2])

    def send_own(role):
        own_out[role] = gather_own[role].reshape(FREQ, PL * AL, 128).astype(bf16)
        send_all(own_out.at[role], own_in.at[role], bins_send.at[role], bins_recv.at[role])

    for chunk in range(8):
        add_headings(chunk)
        if chunk == 0:
            pl.semaphore_wait(barrier, FREQ + 1)
            consts[1].wait()
        core_copy(chunk).start()
        if 1 <= chunk <= 4:
            move_far(chunk - 1)
        if chunk == 4:
            send_late()
            for c in (consts[2], consts[4]):
                c.start()
        if chunk > 4:
            move_own(chunk - 5)
    send_own(0)
    move_own(3)
    send_own(1)
    for c in (consts[2], consts[4]):
        c.wait()

    lane = lax.broadcasted_iota(jnp.int32, (1, 128), 1)
    low = lane < SPOTS
    sign = jnp.where(low, -1.0, 1.0).astype(f32)
    lone = jnp.where(me == 0, 0.0, 1.0).astype(f32)
    ones = jnp.ones((1, 128), f32)

    def masks(p):
        if p > 0:
            return ones, -sign, ones, sign
        return (
            jnp.where(low, ones, lone), jnp.where(low, lone, -ones),
            jnp.where(low, lone, ones), jnp.where(low, -ones, lone),
        )

    def first_pass(bins, count):
        both = jnp.concatenate(
            [bins[:, i * 16 : i * 16 + 16, :].reshape(2 * N, 128) for i in range(count)], axis=1
        )
        for stream in range(2):
            passed[stream, :, : count * 128] = jnp.dot(
                first_v[stream * 2 * N : (stream + 1) * 2 * N, :], both, preferred_element_type=f32
            )

    def twisted(stream, place, block, role, p):
        rows = pl.ds(pl.multiple_of(block * 64, 64), 64)
        more = pl.ds(pl.multiple_of(N + block * 64, 64), 64)
        lanes = slice(place * 128, place * 128 + 128)
        c, s = passed[stream, rows, lanes], passed[stream, more, lanes]
        column = (role * PL + p) * 2
        cw, sw = turn[column, rows, :], turn[column + 1, rows, :]
        return c * cw - s * sw, s * cw + c * sw

    def swap(value):
        return sign * pltpu.roll(value, SPOTS, 1)

    all_but_one(late_in, bins_recv.at[2]).wait()
    first_pass(late_in, LATE)

    @pl.loop(0, 4)
    def _(block):
        values = []
        for i in range(LATE):
            a, b, a_far, b_far = masks(EARLY + i)
            straight, crossed = twisted(0, i, block, 0, EARLY + i)
            straight_far, crossed_far = twisted(1, i, block, 1, EARLY + i)
            value = a * straight + b * straight_far + swap(a_far * crossed + b_far * crossed_far)
            values.append(value.reshape(8, AL, 128))
        times = pl.ds(pl.multiple_of(block * 8, 8), 8)
        cross_out[times] = jnp.concatenate(values, axis=1).astype(bf16)

    cross = pltpu.make_async_remote_copy(
        src_ref=cross_out, dst_ref=cross_in, send_sem=cross_send.at[0],
        recv_sem=cross_recv.at[0], device_id=other_z, device_id_type=MESH,
    )
    cross.start()

    for role in range(2):
        all_but_one(own_in.at[role], bins_recv.at[role]).wait()
        first_pass(own_in.at[role], 2)
        for place in range(2):
            if role == 1 and place == 1:
                cross.wait_recv()

            @pl.loop(0, 4)
            def _(block):
                values = []
                for stream in range(2):
                    p = place * 2 + stream
                    straight, crossed = twisted(stream, place, block, role, p)
                    values.append((masks(p)[role] * straight + swap(masks(p)[2 + role] * crossed)).reshape(8, AL, 128))
                value = jnp.concatenate(values, axis=1)
                times = pl.ds(pl.multiple_of(block * 8, 8), 8)
                rows = slice(place * 16, place * 16 + 16)
                if role == 0:
                    folded[times, rows, :] = value
                else:
                    value += folded[times, rows, :]
                    if place == 1:
                        value += cross_in[times].astype(f32)
                    fold_out[times, rows, :] = value.astype(bf16)

    send_all(fold_out, fold_in, fold_send.at[0], fold_recv.at[0])

    for chunk in range(8):
        core_copy(chunk).wait_send()
    for chunk in range(4):
        pair_copy(chunk).wait_send()
    cross.wait_send()
    for role in range(2):
        all_but_one(own_out.at[role], bins_send.at[role]).wait()
    all_but_one(late_out, bins_send.at[2]).wait()
    all_but_one(fold_in, fold_recv.at[0]).wait()
    all_but_one(fold_out, fold_send.at[0]).wait()


def second_kernel(fold_in, second_v, out, fold_f32, staged, out_sem):
    f32, bf16 = jnp.float32, jnp.bfloat16
    fold_f32[...] = fold_in[...].astype(f32).reshape(FREQ * PL * AL, 128)
    copies = []
    for i in range(2):
        lanes = slice(i * 128, i * 128 + 128)
        table = jnp.concatenate(
            [second_v[:, lanes], second_v[:, N + i * 128 : N + i * 128 + 128]], axis=1
        )
        for t in range(AL):
            value = fold_f32[pl.ds(t, HALF, stride=AL), :].astype(bf16)
            value = jnp.concatenate([value, value], axis=0)
            result = lax.dot_general(
                value, table, (((0,), (0,)), ((), ())), preferred_element_type=f32
            )
            staged[i, pl.ds(t, SPOTS, stride=AL), :] = result[:SPOTS, :128] + result[SPOTS:, 128:]
        copies.append(pltpu.make_async_copy(staged.at[i], out.at[:, lanes], out_sem.at[i]))
        copies[-1].start()
    for copy in copies:
        copy.wait()


def on_device(transfer, amplitudes, weights):
    f32, bf16 = jnp.float32, jnp.bfloat16
    any_spec = pl.BlockSpec(memory_space=pl.ANY)
    first, order, twist, second = [jnp.asarray(table) for table in tables()]
    folded, second = pl.pallas_call(
        kernel,
        out_shape=(pltpu.VMEM((FREQ, PL * AL, 128), bf16), pltpu.VMEM((N, 2 * N), bf16)),
        in_specs=[any_spec, any_spec, pl.BlockSpec(memory_space=pltpu.SMEM)] + [any_spec] * 4,
        out_specs=(pl.BlockSpec(memory_space=pltpu.VMEM),) * 2,
        scratch_shapes=[
            pltpu.VMEM((SLOTS, 2, HEADS, 128, 128), bf16),
            pltpu.VMEM((HEADS, 2, AL * N), f32),
            pltpu.VMEM((2, HEADS, 8, AL * N), f32),
            pltpu.VMEM((2, 8, 4, 128, 128), f32),
            pltpu.VMEM((8, 4, 128, 128), f32),
            pltpu.VMEM((4, 4, FREQ * EARLY, 128), bf16),
            pltpu.VMEM((4, 4, FREQ * EARLY, 128), bf16),
            pltpu.VMEM((2, FREQ * PL * AL, 128), f32),
            pltpu.VMEM((FREQ * LATE * 2 * AL, 128), f32),
            pltpu.VMEM((2, FREQ, PL * AL, 128), bf16),
            pltpu.VMEM((2, FREQ, PL * AL, 128), bf16),
            pltpu.VMEM((FREQ, LATE * 2 * AL, 128), bf16),
            pltpu.VMEM((FREQ, LATE * 2 * AL, 128), bf16),
            pltpu.VMEM((4 * N, 2 * N), bf16),
            pltpu.VMEM((2, HALF, HALF), bf16),
            pltpu.VMEM((N, 128), f32),
            pltpu.VMEM((4 * PL, N, 128), f32),
            pltpu.VMEM((2, 2 * N, 2 * 128), f32),
            pltpu.VMEM((FREQ, PL * AL, 128), f32),
            pltpu.VMEM((FREQ, LATE * AL, 128), bf16),
            pltpu.VMEM((FREQ, LATE * AL, 128), bf16),
            pltpu.VMEM((FREQ, PL * AL, 128), bf16),
            pltpu.SemaphoreType.DMA((SLOTS,)),
            pltpu.SemaphoreType.DMA((5,)),
            pltpu.SemaphoreType.DMA((8,)),
            pltpu.SemaphoreType.DMA((8,)),
            pltpu.SemaphoreType.DMA((4,)),
            pltpu.SemaphoreType.DMA((4,)),
            pltpu.SemaphoreType.DMA((3,)),
            pltpu.SemaphoreType.DMA((3,)),
            pltpu.SemaphoreType.DMA((1,)),
            pltpu.SemaphoreType.DMA((1,)),
            pltpu.SemaphoreType.DMA((1,)),
            pltpu.SemaphoreType.DMA((1,)),
        ],
        compiler_params=pltpu.CompilerParams(
            collective_id=0, has_side_effects=True, vmem_limit_bytes=56 * 2**20
        ),
        cost_estimate=pl.CostEstimate(
            flops=900_000_000, bytes_accessed=22_000_000, transcendentals=0
        ),
    )(transfer, jnp.transpose(amplitudes, (1, 0, 2)), weights, first, order, twist, second)
    stress = pl.pallas_call(
        second_kernel,
        out_shape=jax.ShapeDtypeStruct((SPOTS * AL, N), f32),
        in_specs=[pl.BlockSpec(memory_space=pltpu.VMEM)] * 2,
        out_specs=any_spec,
        scratch_shapes=[
            pltpu.VMEM((FREQ * PL * AL, 128), f32),
            pltpu.VMEM((2, SPOTS * AL, 128), f32),
            pltpu.SemaphoreType.DMA((2,)),
        ],
        cost_estimate=pl.CostEstimate(
            flops=270_000_000, bytes_accessed=1_000_000, transcendentals=0
        ),
    )(*[pltpu.with_memory_space_constraint(v, pltpu.VMEM) for v in (folded, second)])
    return stress.reshape(SPOTS, AL, N)


def solution(mesh):
    in_specs = (P(None, "head", None, "freq"), P(None, "head", "freq"), P("head"))
    out_specs = P("head", "freq", None)
    return jax.shard_map(
        on_device, mesh=mesh, in_specs=in_specs, out_specs=out_specs, check_vma=False
    )
```

```python
import functools
import math

import jax
import jax.numpy as jnp
import ml_dtypes
import numpy as np
from jax import lax
from jax.experimental import pallas as pl
from jax.experimental.pallas import tpu as pltpu
from jax.sharding import PartitionSpec as P

N = 256
HALF = N // 2
HEADS = 9
SPOTS = 64
FREQ = 32
AL = 8
PL = 4
EARLY = 2
LATE = PL - EARLY
SLOTS = 8
MESH = pl.DeviceIdType.MESH


def tables():
    n = np.arange(N)
    angle = 2.0 * math.pi * ((n[:, None] * n[None, :]) % N) / N
    trig = np.stack([np.cos(angle), np.sin(angle)])
    trig = trig.reshape(2, N, FREQ, AL)
    first = np.zeros((2, 2, N, FREQ, 2, AL))
    for i in range(2):
        first[i, :, :, :, i, :] = trig
    first = first.reshape(4 * N, 2 * N).astype(ml_dtypes.bfloat16)
    pairs = HALF // PL * np.arange(PL) + np.arange(FREQ)[:, None]
    order = np.zeros((2, HALF, HALF))
    order[0] = np.eye(HALF)
    order[1][np.arange(HALF), (HALF - np.arange(HALF)) % HALF] = 1.0
    order = order.astype(ml_dtypes.bfloat16)
    pairs = pairs.reshape(-1)
    mirror = np.where(pairs == 0, HALF, N - pairs)
    low = np.stack([pairs, mirror])
    turn = 2.0 * math.pi * ((low[:, :, None] * n) % (N * N)) / (N * N)
    cos_turn, sin_turn = np.cos(turn), np.sin(turn)
    cos_turn[1, 0], sin_turn[1, 0] = -np.sin(turn[1, 0]), np.cos(turn[1, 0])
    twist = np.stack([cos_turn, sin_turn], axis=2)
    twist = twist.reshape(2, FREQ, PL, 2, N).transpose(1, 4, 0, 2, 3).reshape(FREQ, N, 4 * PL)
    wide = np.zeros((FREQ, N, 128), np.float32)
    wide[:, :, : 4 * PL] = twist
    cos_two, sin_two = np.cos(angle)[:HALF], -np.sin(angle)[:HALF]
    sin_two[0] = -((-1.0) ** n)
    second = np.concatenate([cos_two, sin_two], axis=1).astype(np.float32)[pairs]
    upper = second.astype(ml_dtypes.bfloat16)
    lower = (second - upper.astype(np.float32)).astype(ml_dtypes.bfloat16)
    second = np.concatenate([upper, lower], axis=0)
    return first, order, wide, second


def farthest_first():
    steps = [(y, x, z) for y in range(4) for x in range(4) for z in range(2)]
    return sorted(steps, key=lambda d: -(min(d[0], 4 - d[0]) + min(d[1], 4 - d[1]) + d[2]))[:-1]


def kernel(
    transfer, amplitudes, weights, first, order, twist, second,
    fold_in, second_v,
    slabs, amp, wide, part, core_in, pair_out, pair_in, gather_own, gather_late,
    own_out, own_in, late_out, late_in,
    first_v, order_v, twist_v, turn, passed, folded, cross_out, cross_in,
    fold_out,
    slab_sem, const_sem, core_send, core_recv, pair_send, pair_recv,
    bins_send, bins_recv, cross_send, cross_recv, fold_send, fold_recv,
):
    head = lax.axis_index("head")
    me = lax.axis_index("freq")
    z, core = head // 2, lax.rem(head, 2)
    other_core = (z * 2 + 1 - core, me)
    other_z = ((1 - z) * 2 + core, me)
    f32, bf16 = jnp.float32, jnp.bfloat16
    y, x, z_low = me // 8, lax.rem(me // 2, 4), lax.rem(me, 2)
    others = [
        lax.rem(y + dy, 4) * 8 + lax.rem(x + dx, 4) * 2 + lax.rem(z_low + dz, 2)
        for dy, dx, dz in farthest_first()
    ]

    def slab_copy(i):
        far, role, digit = i // 16, lax.rem(i // 8, 2), lax.rem(i, 8)
        half = jnp.where(far == 0, 1 - z, z)
        rows = pl.ds(pl.multiple_of(half * 128, 128), 128)
        lanes = pl.ds(pl.multiple_of(digit * N + role * HALF, 128), 128)
        slot = lax.rem(i, SLOTS)
        return pltpu.make_async_copy(
            transfer.at[:, :, rows, lanes], slabs.at[slot], slab_sem.at[slot]
        )

    consts = [
        pltpu.make_async_copy(amplitudes, amp, const_sem.at[0]),
        pltpu.make_async_copy(order, order_v, const_sem.at[1]),
        pltpu.make_async_copy(first, first_v, const_sem.at[2]),
        pltpu.make_async_copy(twist.at[me], twist_v, const_sem.at[3]),
        pltpu.make_async_copy(second, second_v, const_sem.at[4]),
    ]
    consts[0].start()
    consts[3].start()

    @pl.loop(0, SLOTS)
    def _(i):
        slab_copy(i).start()

    consts[1].start()
    barrier = pltpu.get_barrier_semaphore()
    pl.semaphore_signal(barrier, inc=1, device_id=other_z, device_id_type=MESH)
    pl.semaphore_signal(barrier, inc=1, device_id=other_core, device_id_type=MESH)
    for to in others:
        pl.semaphore_signal(barrier, inc=1, device_id=(head, to), device_id_type=MESH)

    consts[0].wait()
    for r in range(2):
        for h in range(HEADS):
            row = amp[h, r : r + 1, :] * weights[h]
            wide[r, h] = jnp.broadcast_to(row, (8, row.shape[1]))

    consts[3].wait()
    for i in range(4 * PL):
        turn[i] = jnp.broadcast_to(twist_v[:, i : i + 1], (N, 128))

    def add_headings(chunk):
        @pl.loop(0, 4)
        def _(s):
            i = chunk * 4 + s
            role, digit = lax.rem(i // 8, 2), lax.rem(i, 8)
            lanes = pl.ds(pl.multiple_of(digit * N + role * HALF, 128), 128)
            slot = lax.rem(i, SLOTS)
            slab_copy(i).wait()

            @pl.loop(0, 2, unroll=2)
            def _(mine):
                row = jnp.where(mine == 0, 1 - core, core) * SPOTS
                for first_tile in range(0, SPOTS // 16, 4):
                    tiles = range(first_tile, first_tile + 4)
                    sums = [[None, None] for _ in tiles]
                    for h in range(HEADS):
                        wr, wi = wide[0, h, :, lanes][None], wide[1, h, :, lanes][None]
                        for k, tile in enumerate(tiles):
                            rows = pl.ds(pl.multiple_of(row + tile * 16, 16), 16)
                            tr = slabs[slot, 0, h, rows, :].astype(f32).reshape(2, 8, 128)
                            ti = slabs[slot, 1, h, rows, :].astype(f32).reshape(2, 8, 128)
                            re, im = tr * wr - ti * wi, tr * wi + ti * wr
                            sums[k] = [re, im] if h == 0 else [sums[k][0] + re, sums[k][1] + im]
                    for k, tile in enumerate(tiles):
                        for c in range(2):
                            part[mine, chunk, s, pl.ds(c * SPOTS + tile * 16, 16), :] = (
                                sums[k][c].reshape(16, 128)
                            )

            @pl.when(i + SLOTS < 32)
            def _():
                slab_copy(i + SLOTS).start()

    def core_copy(chunk):
        return pltpu.make_async_remote_copy(
            src_ref=part.at[0, chunk], dst_ref=core_in.at[chunk],
            send_sem=core_send.at[chunk], recv_sem=core_recv.at[chunk],
            device_id=other_core, device_id_type=MESH,
        )

    def pair_copy(chunk):
        return pltpu.make_async_remote_copy(
            src_ref=pair_out.at[chunk], dst_ref=pair_in.at[chunk],
            send_sem=pair_send.at[chunk], recv_sem=pair_recv.at[chunk],
            device_id=other_z, device_id_type=MESH,
        )

    def to_rows(table, value):
        return lax.dot_general(
            table, value, (((1,), (1,)), ((), ())), preferred_element_type=f32
        )

    def digit_of(chunk, s):
        return chunk % 2 * 4 + s

    def chip_sum(chunk):
        core_copy(chunk).wait_recv()
        return (part[1, chunk] + core_in[chunk]).reshape(4 * 128, 128)

    def move_far(chunk):
        role = chunk // 2
        moved = to_rows(order_v[role], chip_sum(chunk).astype(bf16))
        for s in range(4):
            slab = moved[:, s * 128 : s * 128 + 128]
            pair_out[chunk, s] = slab[: FREQ * EARLY].astype(bf16)
            for i in range(LATE):
                row = i * 2 * AL + role * AL + digit_of(chunk, s)
                gather_late[pl.ds(row, FREQ, stride=LATE * 2 * AL), :] = slab[
                    FREQ * (EARLY + i) : FREQ * (EARLY + i + 1)
                ]
        pair_copy(chunk).start()

    def move_own(chunk):
        value = chip_sum(4 + chunk)
        upper = value.astype(bf16)
        lower = (value - upper.astype(f32)).astype(bf16)
        role = chunk // 2
        moved = to_rows(order_v[role], upper)
        rest = to_rows(order_v[role, : FREQ * EARLY], lower)
        pair_copy(chunk).wait_recv()
        for s in range(4):
            lanes = slice(s * 128, s * 128 + 128)
            full = moved[: FREQ * EARLY, lanes] + rest[:, lanes] + pair_in[chunk, s].astype(f32)
            for i in range(PL):
                rows = slice(FREQ * i, FREQ * (i + 1))
                gather_own[
                    role, pl.ds(i * AL + digit_of(chunk, s), FREQ, stride=PL * AL), :
                ] = full[rows] if i < EARLY else moved[rows, lanes]

    def send_all(source, landing, send_sem, recv_sem):
        for to in others:
            pltpu.make_async_remote_copy(
                src_ref=source.at[to], dst_ref=landing.at[me],
                send_sem=send_sem, recv_sem=recv_sem,
                device_id=(head, to), device_id_type=MESH,
            ).start()
        landing[me] = source[me]

    def all_but_one(ref, sem):
        return pltpu.make_async_copy(ref.at[pl.ds(0, FREQ - 1)], ref.at[pl.ds(0, FREQ - 1)], sem)

    def send_late():
        late_out[...] = gather_late[...].reshape(FREQ, LATE * 2 * AL, 128).astype(bf16)
        send_all(late_out, late_in, bins_send.at[2], bins_recv.at[2])

    def send_own(role):
        own_out[role] = gather_own[role].reshape(FREQ, PL * AL, 128).astype(bf16)
        send_all(own_out.at[role], own_in.at[role], bins_send.at[role], bins_recv.at[role])

    for chunk in range(8):
        add_headings(chunk)
        if chunk == 0:
            pl.semaphore_wait(barrier, FREQ + 1)
            consts[1].wait()
        core_copy(chunk).start()
        if 1 <= chunk <= 4:
            move_far(chunk - 1)
        if chunk == 4:
            send_late()
            for c in (consts[2], consts[4]):
                c.start()
        if chunk > 4:
            move_own(chunk - 5)
    send_own(0)
    move_own(3)
    send_own(1)
    for c in (consts[2], consts[4]):
        c.wait()

    lane = lax.broadcasted_iota(jnp.int32, (1, 128), 1)
    low = lane < SPOTS
    sign = jnp.where(low, -1.0, 1.0).astype(f32)
    lone = jnp.where(me == 0, 0.0, 1.0).astype(f32)
    ones = jnp.ones((1, 128), f32)

    def masks(p):
        if p > 0:
            return ones, -sign, ones, sign
        return (
            jnp.where(low, ones, lone), jnp.where(low, lone, -ones),
            jnp.where(low, lone, ones), jnp.where(low, -ones, lone),
        )

    def first_pass(bins, count):
        both = jnp.concatenate(
            [bins[:, i * 16 : i * 16 + 16, :].reshape(2 * N, 128) for i in range(count)], axis=1
        )
        for stream in range(2):
            passed[stream, :, : count * 128] = jnp.dot(
                first_v[stream * 2 * N : (stream + 1) * 2 * N, :], both, preferred_element_type=f32
            )

    def twisted(stream, place, block, role, p):
        rows = pl.ds(pl.multiple_of(block * 64, 64), 64)
        more = pl.ds(pl.multiple_of(N + block * 64, 64), 64)
        lanes = slice(place * 128, place * 128 + 128)
        c, s = passed[stream, rows, lanes], passed[stream, more, lanes]
        column = (role * PL + p) * 2
        cw, sw = turn[column, rows, :], turn[column + 1, rows, :]
        return c * cw - s * sw, s * cw + c * sw

    def swap(value):
        return sign * pltpu.roll(value, SPOTS, 1)

    all_but_one(late_in, bins_recv.at[2]).wait()
    first_pass(late_in, LATE)

    @pl.loop(0, 4, unroll=2)
    def _(block):
        values = []
        for i in range(LATE):
            a, b, a_far, b_far = masks(EARLY + i)
            straight, crossed = twisted(0, i, block, 0, EARLY + i)
            straight_far, crossed_far = twisted(1, i, block, 1, EARLY + i)
            value = a * straight + b * straight_far + swap(a_far * crossed + b_far * crossed_far)
            values.append(value.reshape(8, AL, 128))
        times = pl.ds(pl.multiple_of(block * 8, 8), 8)
        cross_out[times] = jnp.concatenate(values, axis=1).astype(bf16)

    cross = pltpu.make_async_remote_copy(
        src_ref=cross_out, dst_ref=cross_in, send_sem=cross_send.at[0],
        recv_sem=cross_recv.at[0], device_id=other_z, device_id_type=MESH,
    )
    cross.start()

    for role in range(2):
        all_but_one(own_in.at[role], bins_recv.at[role]).wait()
        first_pass(own_in.at[role], 2)
        for place in range(2):
            if role == 1 and place == 1:
                cross.wait_recv()

            @pl.loop(0, 4, unroll=2)
            def _(block):
                values = []
                for stream in range(2):
                    p = place * 2 + stream
                    straight, crossed = twisted(stream, place, block, role, p)
                    values.append((masks(p)[role] * straight + swap(masks(p)[2 + role] * crossed)).reshape(8, AL, 128))
                value = jnp.concatenate(values, axis=1)
                times = pl.ds(pl.multiple_of(block * 8, 8), 8)
                rows = slice(place * 16, place * 16 + 16)
                if role == 0:
                    folded[times, rows, :] = value
                else:
                    value += folded[times, rows, :]
                    if place == 1:
                        value += cross_in[times].astype(f32)
                    fold_out[times, rows, :] = value.astype(bf16)

    send_all(fold_out, fold_in, fold_send.at[0], fold_recv.at[0])

    for chunk in range(8):
        core_copy(chunk).wait_send()
    for chunk in range(4):
        pair_copy(chunk).wait_send()
    cross.wait_send()
    for role in range(2):
        all_but_one(own_out.at[role], bins_send.at[role]).wait()
    all_but_one(late_out, bins_send.at[2]).wait()
    all_but_one(fold_in, fold_recv.at[0]).wait()
    all_but_one(fold_out, fold_send.at[0]).wait()


def second_kernel(fold_in, second_v, out, fold_f32, staged, out_sem):
    f32, bf16 = jnp.float32, jnp.bfloat16
    fold_f32[...] = fold_in[...].astype(f32).reshape(FREQ * PL * AL, 128)
    copies = []
    for i in range(2):
        lanes = slice(i * 128, i * 128 + 128)
        table = jnp.concatenate(
            [second_v[:, lanes], second_v[:, N + i * 128 : N + i * 128 + 128]], axis=1
        )
        for t in range(AL):
            value = fold_f32[pl.ds(t, HALF, stride=AL), :].astype(bf16)
            value = jnp.concatenate([value, value], axis=0)
            result = lax.dot_general(
                value, table, (((0,), (0,)), ((), ())), preferred_element_type=f32
            )
            staged[i, pl.ds(t, SPOTS, stride=AL), :] = result[:SPOTS, :128] + result[SPOTS:, 128:]
        copies.append(pltpu.make_async_copy(staged.at[i], out.at[:, lanes], out_sem.at[i]))
        copies[-1].start()
    for copy in copies:
        copy.wait()


def on_device(transfer, amplitudes, weights):
    f32, bf16 = jnp.float32, jnp.bfloat16
    any_spec = pl.BlockSpec(memory_space=pl.ANY)
    first, order, twist, second = [jnp.asarray(table) for table in tables()]
    folded, second = pl.pallas_call(
        kernel,
        out_shape=(pltpu.VMEM((FREQ, PL * AL, 128), bf16), pltpu.VMEM((N, 2 * N), bf16)),
        in_specs=[any_spec, any_spec, pl.BlockSpec(memory_space=pltpu.SMEM)] + [any_spec] * 4,
        out_specs=(pl.BlockSpec(memory_space=pltpu.VMEM),) * 2,
        scratch_shapes=[
            pltpu.VMEM((SLOTS, 2, HEADS, 128, 128), bf16),
            pltpu.VMEM((HEADS, 2, AL * N), f32),
            pltpu.VMEM((2, HEADS, 8, AL * N), f32),
            pltpu.VMEM((2, 8, 4, 128, 128), f32),
            pltpu.VMEM((8, 4, 128, 128), f32),
            pltpu.VMEM((4, 4, FREQ * EARLY, 128), bf16),
            pltpu.VMEM((4, 4, FREQ * EARLY, 128), bf16),
            pltpu.VMEM((2, FREQ * PL * AL, 128), f32),
            pltpu.VMEM((FREQ * LATE * 2 * AL, 128), f32),
            pltpu.VMEM((2, FREQ, PL * AL, 128), bf16),
            pltpu.VMEM((2, FREQ, PL * AL, 128), bf16),
            pltpu.VMEM((FREQ, LATE * 2 * AL, 128), bf16),
            pltpu.VMEM((FREQ, LATE * 2 * AL, 128), bf16),
            pltpu.VMEM((4 * N, 2 * N), bf16),
            pltpu.VMEM((2, HALF, HALF), bf16),
            pltpu.VMEM((N, 128), f32),
            pltpu.VMEM((4 * PL, N, 128), f32),
            pltpu.VMEM((2, 2 * N, 2 * 128), f32),
            pltpu.VMEM((FREQ, PL * AL, 128), f32),
            pltpu.VMEM((FREQ, LATE * AL, 128), bf16),
            pltpu.VMEM((FREQ, LATE * AL, 128), bf16),
            pltpu.VMEM((FREQ, PL * AL, 128), bf16),
            pltpu.SemaphoreType.DMA((SLOTS,)),
            pltpu.SemaphoreType.DMA((5,)),
            pltpu.SemaphoreType.DMA((8,)),
            pltpu.SemaphoreType.DMA((8,)),
            pltpu.SemaphoreType.DMA((4,)),
            pltpu.SemaphoreType.DMA((4,)),
            pltpu.SemaphoreType.DMA((3,)),
            pltpu.SemaphoreType.DMA((3,)),
            pltpu.SemaphoreType.DMA((1,)),
            pltpu.SemaphoreType.DMA((1,)),
            pltpu.SemaphoreType.DMA((1,)),
            pltpu.SemaphoreType.DMA((1,)),
        ],
        compiler_params=pltpu.CompilerParams(
            collective_id=0, has_side_effects=True, vmem_limit_bytes=56 * 2**20
        ),
        cost_estimate=pl.CostEstimate(
            flops=900_000_000, bytes_accessed=22_000_000, transcendentals=0
        ),
    )(transfer, jnp.transpose(amplitudes, (1, 0, 2)), weights, first, order, twist, second)
    stress = pl.pallas_call(
        second_kernel,
        out_shape=jax.ShapeDtypeStruct((SPOTS * AL, N), f32),
        in_specs=[pl.BlockSpec(memory_space=pltpu.VMEM)] * 2,
        out_specs=any_spec,
        scratch_shapes=[
            pltpu.VMEM((FREQ * PL * AL, 128), f32),
            pltpu.VMEM((2, SPOTS * AL, 128), f32),
            pltpu.SemaphoreType.DMA((2,)),
        ],
        cost_estimate=pl.CostEstimate(
            flops=270_000_000, bytes_accessed=1_000_000, transcendentals=0
        ),
    )(*[pltpu.with_memory_space_constraint(v, pltpu.VMEM) for v in (folded, second)])
    return stress.reshape(SPOTS, AL, N)


def solution(mesh):
    in_specs = (P(None, "head", None, "freq"), P(None, "head", "freq"), P("head"))
    out_specs = P("head", "freq", None)
    return jax.shard_map(
        on_device, mesh=mesh, in_specs=in_specs, out_specs=out_specs, check_vma=False
    )
```
